32 devices in a mesh: dp: 4 (over y, core), ctx: 4 (over z), tp: 2 (over x).
Axes of the slice: x: 2, y: 2, z: 4, core: 2. Of those that a mesh axis runs over, the one named last changes fastest.
Arguments:
- tokens: bfloat16 [12288, 2048], P(('dp', 'ctx')), may hold values from -6 to 6
- segments: int32 [12288], P('dp'), may hold values from 0 to 15, as said below
- query_weight: bfloat16 [2048, 2048], P(('dp', 'ctx'), 'tp'), may hold values from -0.125 to 0.125
- key_weight: bfloat16 [2048, 2048], P(('dp', 'ctx'), 'tp'), may hold values from -0.125 to 0.125
- value_weight: bfloat16 [2048, 2048], P(('dp', 'ctx'), 'tp'), may hold values from -0.125 to 0.125
- out_weight: bfloat16 [2048, 2048], P('tp', ('dp', 'ctx')), may hold values from -0.125 to 0.125
- gate_weight: bfloat16 [2048, 8192], P(('dp', 'ctx'), 'tp'), may hold values from -0.125 to 0.125
- up_weight: bfloat16 [2048, 8192], P(('dp', 'ctx'), 'tp'), may hold values from -0.125 to 0.125
- down_weight: bfloat16 [8192, 2048], P('tp', ('dp', 'ctx')), may hold values from -0.0625 to 0.0625
- query_gain: float32 [2048], P('tp'), may hold values from 0.38 to 2.07
- key_gain: float32 [2048], P('tp'), may hold values from 0.38 to 2.07
- attn_gain: float32 [2048], replicated, may hold values from 0.25 to 1.75
- mlp_gain: float32 [2048], replicated, may hold values from 0.25 to 1.75
- cotangent: bfloat16 [12288, 2048], P(('dp', 'ctx')), may hold values from -6 to 6
Outputs:
- output: bfloat16 [12288, 2048], P(('dp', 'ctx'))
- grad_tokens: float32 [12288, 2048], P(('dp', 'ctx'))
- grad_query: float32 [2048, 2048], P(('dp', 'ctx'), 'tp')
- grad_key: float32 [2048, 2048], P(('dp', 'ctx'), 'tp')
- grad_value: float32 [2048, 2048], P(('dp', 'ctx'), 'tp')
- grad_out: float32 [2048, 2048], P('tp', ('dp', 'ctx'))
- grad_gate: float32 [2048, 8192], P(('dp', 'ctx'), 'tp')
- grad_up: float32 [2048, 8192], P(('dp', 'ctx'), 'tp')
- grad_down: float32 [8192, 2048], P('tp', ('dp', 'ctx'))
- grad_query_gain: float32 [2048], P('tp')
- grad_key_gain: float32 [2048], P('tp')
- grad_attn_gain: float32 [2048], replicated
- grad_mlp_gain: float32 [2048], replicated
The draws below stay inside these ranges and needn't reach their ends.
Inputs may be any that keep to these rules, and one draw needn't show every extreme that they name: `segments`: numbers never fall along a sequence and differ between sequences; a sequence holds at most four documents, one of which starts within the first 384 tokens of the sequence and ends within the last 384.
All inputs are finite; a program needn't handle non-finite values.
Results may differ from the reference program's by a relative error of at most 0.023.
Values may be sent and summed in bfloat16 or wider, within the bound.
No kernel may reach another device: no remote copies, remote signals or barrier semaphores. Data moves between devices by JAX's collectives and lax.ppermute only.
A program may use at most 448 MiB of HBM per device.

```python
import jax
import jax.numpy as jnp
from jax import lax

D = 2048
FF = 8192
HD = 128
TOK_DEV = 768
HEADS = 16
SEQ = 3072
TOKENS = 12288
N_DP = 4


def draw_segments(key, part):
    key = jax.random.fold_in(key, 7)
    first_key, second_key, third_key = jax.random.split(key, 3)
    head_len = jax.random.randint(first_key, (N_DP,), 1, TOK_DEV // 2)
    tail_len = jax.random.randint(second_key, (N_DP,), 2, TOK_DEV // 2)
    cut_draw = jax.random.randint(third_key, (N_DP,), 0, 1048576)
    cut_len = cut_draw % (tail_len - 1) + 1
    row_index = jnp.arange(SEQ, dtype=jnp.int32)[None, :]
    local_ids = (row_index >= head_len[:, None]).astype(jnp.int32)
    local_ids = local_ids + (row_index >= SEQ - tail_len[:, None]).astype(jnp.int32)
    local_ids = local_ids + (row_index >= SEQ - tail_len[:, None] + cut_len[:, None]).astype(jnp.int32)
    seq_base = 4 * jnp.arange(N_DP, dtype=jnp.int32)[:, None]
    return (local_ids + seq_base).reshape(-1).astype(jnp.int32)


def gain_ramp(key, low_end, rise):
    column = jnp.arange(D, dtype=jnp.float32) / D
    rough = jax.random.uniform(key, (D,), jnp.float32, 0.85, 1.15)
    return (low_end * rise ** column * rough).astype(jnp.float32)


def draw_query_gain(key, part):
    key = jax.random.fold_in(key, 11)
    return gain_ramp(key, 0.6, 3.0)


def draw_key_gain(key, part):
    key = jax.random.fold_in(key, 13)
    return gain_ramp(key, 0.6, 3.0)


def shard_levels(key, dims, shards, smallest, largest):
    level = 1.0
    for position, parts in shards:
        steps = jax.random.uniform(jax.random.fold_in(jax.random.fold_in(key, 6), position), (parts,), jnp.float32, smallest / len(shards), largest / len(shards))
        level = level * jnp.repeat(jnp.exp(steps), dims[position] // parts).reshape((-1,) + (1,) * (len(dims) - 1 - position))
    return level


def noise(rng, extent, scale, limit, pieces=(), kind=jnp.bfloat16):
    array = scale * jax.random.normal(rng, extent, jnp.float32)
    if pieces:
        array = array * shard_levels(rng, extent, pieces, -0.22, 0.18)
    return jnp.clip(array, -limit, limit).astype(kind)


def setup_inputs(seed: int = 0) -> dict:
    splits = jax.random.split(jax.random.key(seed), 15)
    return {
        "tokens": noise(splits[0], (TOKENS, D), 1.0, 6.0, ((0, 16),)),
        "segments": draw_segments(jax.random.fold_in(splits[14], 71), 0),
        "query_weight": noise(splits[2], (D, D), D ** -0.5, 0.125, ((0, 16), (1, 2))),
        "key_weight": noise(splits[3], (D, D), D ** -0.5, 0.125, ((0, 16), (1, 2))),
        "value_weight": noise(splits[4], (D, D), D ** -0.5, 0.125, ((0, 16), (1, 2))),
        "out_weight": noise(splits[5], (D, D), D ** -0.5, 0.125, ((0, 2), (1, 16))),
        "gate_weight": noise(splits[6], (D, FF), D ** -0.5, 0.125, ((0, 16), (1, 2))),
        "up_weight": noise(splits[7], (D, FF), D ** -0.5, 0.125, ((0, 16), (1, 2))),
        "down_weight": noise(splits[8], (FF, D), FF ** -0.5, 0.0625, ((0, 2), (1, 16))),
        "query_gain": draw_query_gain(jax.random.fold_in(splits[14], 71), 0),
        "key_gain": draw_key_gain(jax.random.fold_in(splits[14], 71), 0),
        "attn_gain": jnp.clip(1.0 + 0.15 * jax.random.normal(splits[11], (D,), jnp.float32), 0.25, 1.75),
        "mlp_gain": jnp.clip(1.0 + 0.15 * jax.random.normal(splits[12], (D,), jnp.float32), 0.25, 1.75),
        "cotangent": noise(splits[13], (TOKENS, D), 1.0, 6.0, ((0, 16),)),
    }


EPSILON = 1e-06
ROPE_BASE = 500000.0
MASKED = -1e+30
HIGHEST = lax.Precision.HIGHEST

@jax.custom_vjp
def low(v):
    return lax.optimization_barrier(v.astype(jnp.bfloat16)).astype(jnp.float32)

@jax.custom_vjp
def low_back(v):
    return v

def low_keep(v):
    return (low(v), None)

def low_pass(kept, grad):
    return (grad,)

def back_keep(v):
    return (v, None)

def back_low(kept, grad):
    return (low(grad),)
low.defvjp(low_keep, low_pass)
low_back.defvjp(back_keep, back_low)

def matmul(left, right):
    return jnp.dot(left, right, precision=HIGHEST, preferred_element_type=jnp.float32)

def rms_scale(values):
    return lax.rsqrt(lax.optimization_barrier(jnp.mean(values * values, axis=-1, keepdims=True)) + EPSILON)

def positions(doc_ids):
    length_all = doc_ids.shape[0]
    row_index = jnp.arange(length_all, dtype=jnp.int32)
    is_start = jnp.concatenate([jnp.ones((1,), dtype=bool), doc_ids[1:] != doc_ids[:-1]])
    starts = jnp.where(is_start, row_index, jnp.zeros_like(row_index))
    return row_index - lax.cummax(starts, axis=0)

def angles(places, head_size):
    frequency = ROPE_BASE ** (-(jnp.arange(head_size // 2, dtype=jnp.float32) * 2.0 / head_size))
    phases = places.astype(jnp.float32)[:, None] * frequency[None, :]
    return (jnp.cos(phases), jnp.sin(phases))

def rotate(values, cosine, sine_rows):
    half_size = values.shape[-1] // 2
    first_half = values[..., :half_size]
    second_half = values[..., half_size:]
    return jnp.concatenate([first_half * cosine - second_half * sine_rows, second_half * cosine + first_half * sine_rows], axis=-1)

def forward_sequence(rows_in, seg_row, query_weight, key_weight, value_weight, out_weight, gate_weight, up_weight, down_weight, query_gain, key_gain, attn_gain, mlp_gain):
    length = rows_in.shape[0]
    query_raw = low_back(matmul(rows_in, query_weight))
    key_raw = low_back(matmul(rows_in, key_weight))
    value_low = low(low_back(matmul(rows_in, value_weight)))
    query_normed = query_raw * rms_scale(query_raw) * query_gain
    key_normed = key_raw * rms_scale(key_raw) * key_gain
    cosine, sine_rows = angles(positions(seg_row), HD)
    query_rot = low(rotate(query_normed.reshape(length, HEADS, HD), cosine[:, None], sine_rows[:, None]))
    key_rot = low(rotate(key_normed.reshape(length, HEADS, HD), cosine[:, None], sine_rows[:, None]))
    value_heads = value_low.reshape(length, HEADS, HD)
    block_rows = min(length, 512)
    blocks = length // block_rows
    row_index = jnp.arange(length, dtype=jnp.int32)
    scaling = HD ** (-0.5)

    def attend(block_args):
        query_block, seg_block, index_block = block_args
        scores = jnp.einsum('qhd,khd->hqk', query_block, key_rot, precision=HIGHEST) * scaling
        scores = low_back(scores)
        allowed = (seg_block[:, None] == seg_row[None, :]) & (row_index[None, :] <= index_block[:, None])
        scores = jnp.where(allowed[None], scores, MASKED)
        row_max = lax.optimization_barrier(jnp.max(scores, axis=-1, keepdims=True))
        exponent = jnp.exp(scores - row_max)
        softmax_rows = exponent / lax.optimization_barrier(jnp.sum(exponent, axis=-1, keepdims=True))
        return jnp.einsum('hqk,khd->qhd', low(softmax_rows), value_heads, precision=HIGHEST)
    attended = lax.map(jax.checkpoint(attend), (query_rot.reshape(blocks, block_rows, HEADS, HD), seg_row.reshape(blocks, block_rows), row_index.reshape(blocks, block_rows)))
    attended = low(low_back(attended.reshape(length, D)))
    attn_rows = low_back(matmul(attended, out_weight))
    hidden_rows = rows_in + attn_rows * rms_scale(attn_rows) * attn_gain
    hidden_low = low(hidden_rows)
    gate_rows = low_back(matmul(hidden_low, gate_weight))
    up_rows = low_back(matmul(hidden_low, up_weight))
    activation = low(jax.nn.silu(gate_rows) * up_rows)
    mlp_rows = low_back(matmul(activation, down_weight))
    return hidden_rows + mlp_rows * rms_scale(mlp_rows) * mlp_gain

def reference(tokens, segments, query_weight, key_weight, value_weight, out_weight, gate_weight, up_weight, down_weight, query_gain, key_gain, attn_gain, mlp_gain, cotangent):
    params = tuple((weight.astype(jnp.float32) for weight in (query_weight, key_weight, value_weight, out_weight, gate_weight, up_weight, down_weight, query_gain, key_gain, attn_gain, mlp_gain)))
    inputs = tokens.astype(jnp.float32).reshape(N_DP, SEQ, D)
    upstream = cotangent.astype(jnp.float32).reshape(N_DP, SEQ, D)
    doc_ids = segments.reshape(N_DP, SEQ)

    def sequence_step(totals, item):
        rows_in, seg_row, grad_rows = item

        def closed(rows_arg, *weights):
            return forward_sequence(rows_arg, seg_row, *weights)
        result, pull = jax.vjp(closed, rows_in, *params)
        grads = pull(grad_rows)
        new_totals = tuple((earlier + extra for earlier, extra in zip(totals, grads[1:])))
        return (new_totals, (result, grads[0]))
    zero_totals = tuple((jnp.zeros_like(weight) for weight in params))
    totals, (results, input_grads) = lax.scan(sequence_step, zero_totals, (inputs, doc_ids, upstream))
    return (results.reshape(TOKENS, D).astype(jnp.bfloat16), input_grads.reshape(TOKENS, D), totals[0], totals[1], totals[2], totals[3], totals[4], totals[5], totals[6], totals[7], totals[8], totals[9], totals[10])
```

```python
import functools
import math

import jax
import jax.numpy as jnp
from jax import lax
from jax.experimental import pallas as pl
from jax.experimental.pallas import tpu as pltpu
from jax.sharding import Mesh
from jax.sharding import PartitionSpec as P

HD = 128
EPSILON = 1e-06
ROPE_BASE = 500000.0
MASKED = -1e30
SCALING = HD**-0.5
LOG2E = math.log2(math.e)
BLOCK_K = 256
VMEM_LIMIT = 48 << 20
bf16 = jnp.bfloat16
f32 = jnp.float32


def cost(products, moved):
    return pl.CostEstimate(flops=products, bytes_accessed=moved // 2, transcendentals=0)


def dims(left, right, over):
    return lax.dot_general(left, right, (over, ((), ())), preferred_element_type=f32)


def product(left, right):
    return dims(left, right, ((1,), (0,)))


def contract_rows(left, right):
    return dims(left, right, ((0,), (0,)))


def contract_cols(left, right):
    return dims(left, right, ((1,), (1,)))


def key_steps(block, low, high, bk, per_block):
    end = block * per_block
    begin = jnp.minimum(low // bk, end)
    clear = jnp.minimum((high + bk - 1) // bk, end)
    return begin, clear, end


def diagonal(step, scores, start, first, bk):
    key = step * bk + lax.broadcasted_iota(jnp.int32, scores.shape, 0)
    place = step * bk + lax.broadcasted_iota(jnp.int32, scores.shape, 1)
    return jnp.where((key <= place) & (key + first >= start), scores, MASKED)


def attend_kernel(
    first_ref, low_ref, high_ref, start_ref, q_ref, k_ref, v_ref, o_ref, lse_ref, *, bk
):
    size = q_ref.shape[0]
    per_block = size // bk
    block = first_ref[0] + pl.program_id(2)
    sequence = pl.program_id(1)
    queries = q_ref[...]
    start = start_ref[0]

    def update(carry, scores, values):
        peak, total, acc = carry
        new_peak = jnp.maximum(peak, jnp.max(scores, axis=0, keepdims=True))
        weights = jnp.exp2(scores - new_peak)
        shrink = jnp.exp2(peak - new_peak)
        total = total * shrink + jnp.sum(weights, axis=0, keepdims=True)
        acc = acc * shrink + contract_rows(values, weights.astype(bf16))
        return new_peak, total, acc

    def clear_step(j, carry):
        rows = pl.ds(pl.multiple_of(j * bk, bk), bk)
        return update(carry, contract_cols(k_ref[rows, :], queries), v_ref[rows, :])

    def masked_step(j, carry):
        rows = pl.ds(pl.multiple_of(j * bk, bk), bk)
        scores = contract_cols(k_ref[rows, :], queries)
        key = j * bk + lax.broadcasted_iota(jnp.int32, (bk, 1), 0)
        return update(carry, jnp.where(key >= start, scores, MASKED), v_ref[rows, :])

    begin, clear, end = key_steps(
        block, low_ref[sequence, block], high_ref[sequence, block], bk, per_block
    )
    carry = (
        jnp.full((1, size), MASKED, f32),
        jnp.zeros((1, size), f32),
        jnp.zeros((HD, size), f32),
    )
    carry = lax.fori_loop(begin, clear, masked_step, carry)
    carry = lax.fori_loop(jnp.maximum(begin, clear), end, clear_step, carry)
    for step in range(per_block):
        cut = step * bk
        rows = pl.ds(pl.multiple_of(block * size + cut, bk), bk)
        scores = contract_cols(k_ref[rows, :], queries[cut:])
        scores = diagonal(step, scores, start[:, cut:], block * size, bk)
        right = update(tuple(part[:, cut:] for part in carry), scores, v_ref[rows, :])
        if cut:
            right = tuple(
                jnp.concatenate([part[:, :cut], new], axis=1) for part, new in zip(carry, right)
            )
        carry = right
    peak, total, acc = carry
    o_ref[...] = (acc / total).T.astype(bf16)
    lse_ref[0] = peak + jnp.log2(total)


def attend(first, starts, edges, heads, size, query, key, value):
    sequences, length = starts.shape
    slots = query[0].shape[0] // (sequences * size)
    rows = query[0].shape[0]

    def part(offset):
        return pl.BlockSpec((size, HD), lambda g, b, s, *refs: (b * slots + s, offset + g))

    def whole(offset):
        return pl.BlockSpec((length, HD), lambda g, b, s, *refs: (b, offset + g))

    return pl.pallas_call(
        functools.partial(attend_kernel, bk=min(BLOCK_K, size)),
        grid_spec=pltpu.PrefetchScalarGridSpec(
            num_scalar_prefetch=3,
            grid=(heads, sequences, slots),
            in_specs=[
                pl.BlockSpec((1, 1, size), lambda g, b, s, first, *refs: (b, 0, first[0] + s)),
                part(query[1]),
                whole(key[1]),
                whole(value[1]),
            ],
            out_specs=[
                part(0),
                pl.BlockSpec((1, 1, size), lambda g, b, s, *refs: (g, 0, b * slots + s)),
            ],
        ),
        out_shape=[
            jax.ShapeDtypeStruct((rows, heads * HD), bf16),
            jax.ShapeDtypeStruct((heads, 1, rows), f32),
        ],
        cost_estimate=cost(4 * HD * heads * rows * length, 0),
        compiler_params=pltpu.CompilerParams(vmem_limit_bytes=VMEM_LIMIT),
        name="attend",
    )(first, *edges, starts[:, None, :], query[0], key[0], value[0])


def attend_back_kernel(
    first_ref,
    low_ref,
    high_ref,
    start_ref,
    lse_ref,
    q_ref,
    o_ref,
    do_ref,
    k_ref,
    v_ref,
    dq_ref,
    dk_ref,
    dv_ref,
    dk_sum,
    dv_sum,
    *,
    bk,
):
    size = q_ref.shape[0]
    per_block = size // bk
    block = first_ref[0] + pl.program_id(2)
    sequence = pl.program_id(1)
    queries = q_ref[...]
    grads = do_ref[...]
    start = start_ref[0]
    lse = lse_ref[0]
    delta = jnp.sum((grads.astype(f32) * o_ref[...].astype(f32)).T, axis=0, keepdims=True)

    @pl.when(pl.program_id(2) == 0)
    def _():
        dk_sum[...] = jnp.zeros_like(dk_sum)
        dv_sum[...] = jnp.zeros_like(dv_sum)

    def update(dq, scores, rows, cut):
        probs = jnp.exp2(scores - lse[:, cut:])
        dv_sum[rows, :] += product(probs.astype(bf16), grads[cut:])
        dprobs = contract_cols(v_ref[rows, :], grads[cut:])
        dscores = (probs * (dprobs - delta[:, cut:])).astype(bf16)
        dk_sum[rows, :] += product(dscores, queries[cut:])
        return dq + contract_rows(k_ref[rows, :], dscores)

    def clear_step(j, dq):
        rows = pl.ds(pl.multiple_of(j * bk, bk), bk)
        return update(dq, contract_cols(k_ref[rows, :], queries), rows, 0)

    def masked_step(j, dq):
        rows = pl.ds(pl.multiple_of(j * bk, bk), bk)
        scores = contract_cols(k_ref[rows, :], queries)
        key = j * bk + lax.broadcasted_iota(jnp.int32, (bk, 1), 0)
        return update(dq, jnp.where(key >= start, scores, MASKED), rows, 0)

    begin, clear, end = key_steps(
        block, low_ref[sequence, block], high_ref[sequence, block], bk, per_block
    )
    dq = jnp.zeros((HD, size), f32)
    dq = lax.fori_loop(begin, clear, masked_step, dq)
    dq = lax.fori_loop(jnp.maximum(begin, clear), end, clear_step, dq)
    for step in range(per_block):
        cut = step * bk
        rows = pl.ds(pl.multiple_of(block * size + cut, bk), bk)
        scores = contract_cols(k_ref[rows, :], queries[cut:])
        scores = diagonal(step, scores, start[:, cut:], block * size, bk)
        right = update(dq[:, cut:], scores, rows, cut)
        dq = jnp.concatenate([dq[:, :cut], right], axis=1) if cut else right
    dq_ref[...] = (dq.T * SCALING).astype(bf16)

    @pl.when(pl.program_id(2) == pl.num_programs(2) - 1)
    def _():
        dk_ref[...] = (dk_sum[...] * (1.0 / LOG2E)).astype(bf16)
        dv_ref[...] = dv_sum[...].astype(bf16)


def attend_back(first, starts, edges, heads, size, lse, query, out, grad, key, value):
    sequences, length = starts.shape
    rows = query[0].shape[0]
    slots = rows // (sequences * size)

    def part(offset):
        return pl.BlockSpec((size, HD), lambda g, b, s, *refs: (b * slots + s, offset + g))

    def whole(offset):
        return pl.BlockSpec((length, HD), lambda g, b, s, *refs: (b, offset + g))

    return pl.pallas_call(
        functools.partial(attend_back_kernel, bk=min(BLOCK_K, size)),
        grid_spec=pltpu.PrefetchScalarGridSpec(
            num_scalar_prefetch=3,
            grid=(heads, sequences, slots),
            in_specs=[
                pl.BlockSpec((1, 1, size), lambda g, b, s, first, *refs: (b, 0, first[0] + s)),
                pl.BlockSpec((1, 1, size), lambda g, b, s, *refs: (g, 0, b * slots + s)),
                part(query[1]),
                part(0),
                part(0),
                whole(key[1]),
                whole(value[1]),
            ],
            out_specs=[part(0), whole(0), whole(0)],
            scratch_shapes=[pltpu.VMEM((length, HD), f32)] * 2,
        ),
        out_shape=[
            jax.ShapeDtypeStruct((rows, heads * HD), bf16),
            jax.ShapeDtypeStruct((sequences * length, heads * HD), bf16),
            jax.ShapeDtypeStruct((sequences * length, heads * HD), bf16),
        ],
        cost_estimate=cost(5 * HD * heads * rows * length, 0),
        compiler_params=pltpu.CompilerParams(vmem_limit_bytes=VMEM_LIMIT),
        name="attend_back",
    )(first, *edges, starts[:, None, :], lse, query[0], out, grad, key[0], value[0])


def turn_kernel(place_ref, raw_ref, scale_ref, gain_ref, cos_ref, sin_ref, out_ref, *, heads):
    for c in range(3):
        for h in range(heads):
            cols = slice((c * heads + h) * HD, (c * heads + h + 1) * HD)
            values = raw_ref[:, cols]
            if c < 2:
                values = values * scale_ref[c] * gain_ref[c, :, h * HD : (h + 1) * HD]
                values = values * cos_ref[...] + pltpu.roll(values, HD // 2, 1) * sin_ref[...]
            if c == 0:
                values = values * (SCALING * LOG2E)
            out_ref[:, cols] = values.astype(bf16)


def turn(place, raw, scales, gains, cosine, sine, heads):
    rows = raw.shape[0]
    size = rows // place.shape[0]
    return pl.pallas_call(
        functools.partial(turn_kernel, heads=heads),
        grid_spec=pltpu.PrefetchScalarGridSpec(
            num_scalar_prefetch=1,
            grid=(rows // size,),
            in_specs=[
                pl.BlockSpec((size, 3 * heads * HD), lambda i, place: (place[i], 0)),
                pl.BlockSpec((2, size, 1), lambda i, place: (0, i, 0)),
                pl.BlockSpec((2, 1, heads * HD), lambda i, place: (0, 0, 0)),
                pl.BlockSpec((size, HD), lambda i, place: (i, 0)),
                pl.BlockSpec((size, HD), lambda i, place: (i, 0)),
            ],
            out_specs=pl.BlockSpec((size, 3 * heads * HD), lambda i, place: (i, 0)),
        ),
        out_shape=jax.ShapeDtypeStruct(raw.shape, bf16),
        cost_estimate=cost(0, 20 * rows * heads * HD),
        compiler_params=pltpu.CompilerParams(vmem_limit_bytes=VMEM_LIMIT),
        name="turn",
    )(place, raw, scales, gains, cosine, sine)


def unturn_kernel(
    place_ref,
    dq_ref,
    dk_ref,
    raw_ref,
    scale_ref,
    gain_ref,
    cos_ref,
    sin_ref,
    out_ref,
    inner_ref,
    sum_ref,
    *,
    heads,
):
    @pl.when(pl.program_id(0) == 0)
    def _():
        sum_ref[...] = jnp.zeros_like(sum_ref)

    for c, grad_ref in enumerate((dq_ref, dk_ref)):
        inner = 0.0
        for h in range(heads):
            head = slice(h * HD, (h + 1) * HD)
            cols = slice((c * heads + h) * HD, (c * heads + h + 1) * HD)
            grad = grad_ref[:, head].astype(f32)
            normed = grad * cos_ref[...] - pltpu.roll(grad, HD // 2, 1) * sin_ref[...]
            unit = raw_ref[:, cols] * scale_ref[c]
            scaled = normed * gain_ref[c, :, head]
            out_ref[:, cols] = scaled
            inner = inner + jnp.sum(scaled * unit, axis=1, keepdims=True)
            sum_ref[c, :, head] += jnp.sum(normed * unit, axis=0, keepdims=True)
        inner_ref[c] = inner


def unturn(place, dq, dk, raw, scales, gains, cosine, sine, heads):
    rows = raw.shape[0]
    size = rows // place.shape[0]
    width = heads * HD
    return pl.pallas_call(
        functools.partial(unturn_kernel, heads=heads),
        grid_spec=pltpu.PrefetchScalarGridSpec(
            num_scalar_prefetch=1,
            grid=(rows // size,),
            in_specs=[
                pl.BlockSpec((size, width), lambda i, place: (i, 0)),
                pl.BlockSpec((size, width), lambda i, place: (i, 0)),
                pl.BlockSpec((size, 3 * width), lambda i, place: (place[i], 0)),
                pl.BlockSpec((2, size, 1), lambda i, place: (0, i, 0)),
                pl.BlockSpec((2, 1, width), lambda i, place: (0, 0, 0)),
                pl.BlockSpec((size, HD), lambda i, place: (i, 0)),
                pl.BlockSpec((size, HD), lambda i, place: (i, 0)),
            ],
            out_specs=[
                pl.BlockSpec((size, 2 * width), lambda i, place: (i, 0)),
                pl.BlockSpec((2, size, 1), lambda i, place: (0, i, 0)),
                pl.BlockSpec((2, 1, width), lambda i, place: (0, 0, 0)),
            ],
        ),
        out_shape=[
            jax.ShapeDtypeStruct((rows, 2 * width), f32),
            jax.ShapeDtypeStruct((2, rows, 1), f32),
            jax.ShapeDtypeStruct((2, 1, width), f32),
        ],
        cost_estimate=cost(0, 32 * rows * width),
        compiler_params=pltpu.CompilerParams(vmem_limit_bytes=VMEM_LIMIT),
        name="unturn",
    )(place, dq, dk, raw, scales, gains, cosine, sine)


def norm_back_kernel(
    place_ref, scaled_ref, raw_ref, scale_ref, inner_ref, dv_ref, out_ref, *, heads
):
    width = heads * HD
    for c in range(2):
        cols = slice(c * width, (c + 1) * width)
        unit = raw_ref[:, cols] * scale_ref[c]
        out_ref[:, cols] = (scale_ref[c] * (scaled_ref[:, cols] - unit * inner_ref[c])).astype(bf16)
    out_ref[:, 2 * width :] = dv_ref[...]


def norm_back(place, scaled, raw, scales, inner, dv, heads):
    rows = raw.shape[0]
    size = rows // place.shape[0]
    width = heads * HD
    return pl.pallas_call(
        functools.partial(norm_back_kernel, heads=heads),
        grid_spec=pltpu.PrefetchScalarGridSpec(
            num_scalar_prefetch=1,
            grid=(rows // size,),
            in_specs=[
                pl.BlockSpec((size, 2 * width), lambda i, place: (i, 0)),
                pl.BlockSpec((size, 3 * width), lambda i, place: (place[i], 0)),
                pl.BlockSpec((2, size, 1), lambda i, place: (0, i, 0)),
                pl.BlockSpec((2, size, 1), lambda i, place: (0, i, 0)),
                pl.BlockSpec((size, width), lambda i, place: (i, 0)),
            ],
            out_specs=pl.BlockSpec((size, 3 * width), lambda i, place: (place[i], 0)),
        ),
        out_shape=jax.ShapeDtypeStruct((rows, 3 * width), bf16),
        cost_estimate=cost(0, 24 * rows * width),
        compiler_params=pltpu.CompilerParams(vmem_limit_bytes=VMEM_LIMIT),
        name="norm_back",
    )(place, scaled, raw, scales, inner, dv)


def reorder_kernel(in_ref, out_ref, *, order):
    size = in_ref.shape[1] // len(order)
    for n, m in enumerate(order):
        out_ref[:, n * size : (n + 1) * size] = in_ref[:, m * size : (m + 1) * size]


def reorder(values, order):
    rows, width = values.shape
    size = math.gcd(rows, 192)
    spec = pl.BlockSpec((size, width), lambda i: (i, 0))
    return pl.pallas_call(
        functools.partial(reorder_kernel, order=order),
        grid=(rows // size,),
        in_specs=[spec],
        out_specs=spec,
        out_shape=jax.ShapeDtypeStruct(values.shape, values.dtype),
        cost_estimate=cost(0, 2 * values.size * values.dtype.itemsize),
        compiler_params=pltpu.CompilerParams(vmem_limit_bytes=VMEM_LIMIT),
        name="reorder",
    )(values)


def outer_kernel(left_a, left_b, right_a, right_b, out_ref):
    total = contract_rows(left_a[...], right_a[...]) + contract_rows(left_b[...], right_b[...])
    out_ref[...] = total.astype(bf16)


def outer(lefts, rights):
    rows, high = lefts[0].shape
    wide = rights[0].shape[1]
    tall, broad = math.gcd(high, 512), math.gcd(wide, 1024)
    left = pl.BlockSpec((rows, tall), lambda i, j: (0, i))
    right = pl.BlockSpec((rows, broad), lambda i, j: (0, j))
    return pl.pallas_call(
        outer_kernel,
        grid=(high // tall, wide // broad),
        in_specs=[left, left, right, right],
        out_specs=pl.BlockSpec((tall, broad), lambda i, j: (i, j)),
        out_shape=jax.ShapeDtypeStruct((high, wide), bf16),
        cost_estimate=cost(2 * rows * high * wide, 0),
        compiler_params=pltpu.CompilerParams(vmem_limit_bytes=VMEM_LIMIT),
        name="outer",
    )(*lefts, *rights)


def feed_kernel(hidden_ref, gate_ref, up_ref, gate_out, up_out, act_out):
    gate = product(hidden_ref[...], gate_ref[...])
    up = product(hidden_ref[...], up_ref[...])
    gate_out[...] = gate.astype(bf16)
    up_out[...] = up.astype(bf16)
    act_out[...] = (gate * jax.nn.sigmoid(gate) * up).astype(bf16)


def feed(hidden, gate_up):
    rows, width = hidden.shape
    units = gate_up.shape[1] // 2
    wide = math.gcd(units, 512)
    count = units // wide
    out = pl.BlockSpec((rows, wide), lambda j: (0, j))
    return pl.pallas_call(
        feed_kernel,
        grid=(count,),
        in_specs=[
            pl.BlockSpec((rows, width), lambda j: (0, 0)),
            pl.BlockSpec((width, wide), lambda j: (0, j)),
            pl.BlockSpec((width, wide), lambda j: (0, count + j)),
        ],
        out_specs=[out, out, out],
        out_shape=[jax.ShapeDtypeStruct((rows, units), bf16)] * 3,
        cost_estimate=cost(2 * rows * width * units, 0),
        compiler_params=pltpu.CompilerParams(vmem_limit_bytes=VMEM_LIMIT),
        name="feed",
    )(hidden, gate_up, gate_up)


def project_kernel(left_ref, right_ref, out_ref):
    out_ref[...] = contract_cols(left_ref[...], right_ref[...]).astype(bf16)


def project(left, right):
    rows, units = left.shape
    width = right.shape[0]
    wide = math.gcd(width, 512)
    return pl.pallas_call(
        project_kernel,
        grid=(width // wide,),
        in_specs=[
            pl.BlockSpec((rows, units), lambda j: (0, 0)),
            pl.BlockSpec((wide, units), lambda j: (j, 0)),
        ],
        out_specs=pl.BlockSpec((rows, wide), lambda j: (0, j)),
        out_shape=jax.ShapeDtypeStruct((rows, width), bf16),
        cost_estimate=cost(rows * units * width, 0),
        compiler_params=pltpu.CompilerParams(vmem_limit_bytes=VMEM_LIMIT),
        name="project",
    )(left, right)


def feed_back_kernel(grad_ref, down_ref, gate_ref, up_ref, gate_out, up_out):
    grad = product(grad_ref[...], down_ref[...])
    gate = gate_ref[...].astype(f32)
    sigmoid = jax.nn.sigmoid(gate)
    gate_out[...] = (
        grad * up_ref[...].astype(f32) * (sigmoid * (1.0 + gate * (1.0 - sigmoid)))
    ).astype(bf16)
    up_out[...] = (grad * (gate * sigmoid)).astype(bf16)


def feed_back(grad, down, gate, up):
    rows, width = grad.shape
    units = down.shape[1]
    wide = math.gcd(units, 512)
    part = pl.BlockSpec((rows, wide), lambda j: (0, j))
    return pl.pallas_call(
        feed_back_kernel,
        grid=(units // wide,),
        in_specs=[
            pl.BlockSpec((rows, width), lambda j: (0, 0)),
            pl.BlockSpec((width, wide), lambda j: (0, j)),
            part,
            part,
        ],
        out_specs=[part, part],
        out_shape=[jax.ShapeDtypeStruct((rows, units), bf16)] * 2,
        cost_estimate=cost(rows * width * units, 0),
        compiler_params=pltpu.CompilerParams(vmem_limit_bytes=VMEM_LIMIT),
        name="feed_back",
    )(grad, down, gate, up)


def project_both_kernel(gate_grad, up_grad, gate_ref, up_ref, out_ref):
    total = contract_cols(gate_grad[...], gate_ref[...]) + contract_cols(up_grad[...], up_ref[...])
    out_ref[...] = total.astype(bf16)


def project_both(gate_grad, up_grad, gate_up):
    rows, units = gate_grad.shape
    width = gate_up.shape[0]
    wide = math.gcd(width, 512)
    left = pl.BlockSpec((rows, units), lambda j: (0, 0))
    return pl.pallas_call(
        project_both_kernel,
        grid=(width // wide,),
        in_specs=[
            left,
            left,
            pl.BlockSpec((wide, units), lambda j: (j, 0)),
            pl.BlockSpec((wide, units), lambda j: (j, 1)),
        ],
        out_specs=pl.BlockSpec((rows, wide), lambda j: (0, j)),
        out_shape=jax.ShapeDtypeStruct((rows, width), bf16),
        cost_estimate=cost(2 * rows * units * width, 0),
        compiler_params=pltpu.CompilerParams(vmem_limit_bytes=VMEM_LIMIT),
        name="project_both",
    )(gate_grad, up_grad, gate_up, gate_up)


def tie_kernel(*refs):
    pass


def tie(values, *others):
    return pl.pallas_call(
        tie_kernel,
        in_specs=[pl.BlockSpec(memory_space=pl.ANY)] * (1 + len(others)),
        out_specs=pl.BlockSpec(memory_space=pl.ANY),
        out_shape=jax.ShapeDtypeStruct(values.shape, values.dtype),
        input_output_aliases={0: 0},
        cost_estimate=cost(0, 0),
        name="tie",
    )(values, *others)


def doc_starts(doc_ids):
    row_index = jnp.arange(doc_ids.shape[-1], dtype=jnp.int32)
    is_start = jnp.concatenate(
        [jnp.ones_like(doc_ids[:, :1], dtype=bool), doc_ids[:, 1:] != doc_ids[:, :-1]], axis=1
    )
    return lax.cummax(jnp.where(is_start, row_index[None, :], 0), axis=1)


def angles(places):
    frequency = ROPE_BASE ** (-(jnp.arange(HD // 2, dtype=f32) * 2.0 / HD))
    phases = places.astype(f32)[:, None] * frequency[None, :]
    cosine, sine = jnp.cos(phases), jnp.sin(phases)
    return (
        jnp.concatenate([cosine, cosine], axis=-1),
        jnp.concatenate([-sine, sine], axis=-1),
    )


def swap(values, axis):
    return lax.ppermute(values, axis, [(0, 1), (1, 0)])


def shift_ctx(values, steps, size):
    return lax.ppermute(values, "ctx", [(i, (i + steps) % size) for i in range(size)])


def by_source(received, me):
    size = len(received)
    turned = jnp.stack(received[::-1] + received[::-1])
    return lax.dynamic_slice_in_dim(turned, size - 1 - me, size, axis=0)


def in_order(index, mine, theirs):
    return jnp.where(index == 0, jnp.stack([mine, theirs]), jnp.stack([theirs, mine]))


def beside(index, mine, theirs):
    first = jnp.where(index == 0, mine, theirs)
    second = jnp.where(index == 0, theirs, mine)
    return jnp.concatenate([first, second], axis=1)


def lowered(values):
    return lax.reduce_precision(values, 8, 7).astype(bf16)


def body(
    tokens,
    segments,
    query_weight,
    key_weight,
    value_weight,
    out_weight,
    gate_weight,
    up_weight,
    down_weight,
    query_gain,
    key_gain,
    attn_gain,
    mlp_gain,
    cotangent,
    *,
    sizes,
):
    core = lax.axis_index("core")
    ctx = lax.axis_index("ctx")
    here_y = lax.axis_index("y")
    here_x = lax.axis_index("tp")
    n_ctx, n_tp = sizes["ctx"], sizes["tp"]
    rows, width = tokens.shape
    piece = query_weight.shape[0]
    local = query_weight.shape[1]
    att = local // 2
    half = width // 2
    short = rows // 2

    def column_half(values, index):
        size = values.shape[1] // 2
        return lax.dynamic_slice_in_dim(values, index * size, size, axis=1)

    def number(y, c, z):
        return (y * 2 + c) * n_ctx + z

    inward = [number(y, c, z) for y in range(2) for z in range(n_ctx) for c in range(2)]
    outward = [inward.index(n) for n in range(4 * n_ctx)]

    def gather(*shards, after=()):
        mine = jnp.concatenate([column_half(shard, core) for shard in shards], axis=1)
        theirs = jnp.concatenate([column_half(shard, 1 - core) for shard in shards], axis=1)
        pair = in_order(core, mine, swap(theirs, "core")).reshape(2 * piece, -1)
        if after:
            pair = tie(pair, *after)
        return lax.all_gather(pair, ("y", "ctx"), axis=0, tiled=True)

    def scatter(grad):
        return lax.psum_scatter(grad, ("y", "ctx"), scatter_dimension=0, tiled=True)

    def own_share(low):
        mine = lax.dynamic_slice_in_dim(low, core * piece, piece)
        theirs = swap(lax.dynamic_slice_in_dim(low, (1 - core) * piece, piece), "core")
        return beside(core, mine, theirs).astype(f32)

    def both(values):
        return jnp.concatenate([values, swap(values, "core")], axis=0)

    def open_sum(part):
        part = part.reshape(2, -1, width)
        total = part[0].astype(f32) + swap(part[1], "core").astype(f32)
        if n_tp == 2:
            low = lowered(total)
            return low, swap(low, "tp")
        low = lax.psum(total.astype(bf16), "tp")
        return low, jnp.zeros_like(low)

    def close_sum(low, other):
        return low.astype(f32) + other.astype(f32)

    def chunk(values, j):
        split = values.reshape(2, rows, -1)[:, j * short : (j + 1) * short]
        return split.reshape(2 * short, -1)

    def unchunk(parts):
        split = [part.reshape(2, short, -1) for part in parts]
        return jnp.concatenate(split, axis=1).reshape(2 * rows, -1)

    by_sequence = n_tp == 2 and (local // HD) % n_ctx == 0
    out_all = gather(out_weight.T)
    inner_tokens = reorder(tokens, inward)
    inner_cotangent = reorder(cotangent, inward)
    attn_gain, mlp_gain = (
        jnp.concatenate([gain[n * piece : (n + 1) * piece] for n in inward])
        for gain in (attn_gain, mlp_gain)
    )

    if by_sequence:
        heads = local // HD // n_ctx
        wide = heads * HD

        def shard_columns(index):
            return jnp.concatenate(
                [
                    lax.dynamic_slice_in_dim(shard, index * wide, wide, axis=1)
                    for shard in (query_weight, key_weight, value_weight)
                ],
                axis=1,
            )

        columns = [shard_columns(ctx)]
        for step in range(1, n_ctx):
            columns.append(shift_ctx(shard_columns(lax.rem(ctx + step, n_ctx)), step, n_ctx))
        weight = by_source(columns, ctx).reshape(n_ctx * piece, 3 * wide)
        weight = in_order(core, weight, swap(weight, "core")).reshape(half, 3 * wide)
        weight = in_order(here_y, weight, swap(weight, "y")).reshape(width, 3 * wide)

        sent = lax.dynamic_slice_in_dim(tokens, here_x * short, short)
        blocks = []
        for step in range(1, n_ctx):
            sent = shift_ctx(sent, 1, n_ctx)
            if step == 1:
                sent = tie(sent, *columns[1:])
            blocks.append(in_order(here_x, sent, swap(sent, "tp")).reshape(rows, width))
        blocks.append(tokens)
        raws = [product(block, weight) for block in blocks]
        raw = jnp.concatenate(raws)
        sums = [
            jnp.stack(
                [jnp.sum(jnp.square(r[:, c * wide : (c + 1) * wide]), axis=-1) for c in range(2)]
            )
            for r in raws
        ]
        squares = by_source([sums[-1]] + sums[:-1], ctx).swapaxes(0, 1).reshape(2, n_ctx * rows)
        size = math.gcd(rows, 384)
        order = jnp.arange(n_ctx * rows // size, dtype=jnp.int32)
        block_of, inside = order // (rows // size), order % (rows // size)
        place = lax.rem(ctx - block_of - 1 + n_ctx, n_ctx) * (rows // size) + inside
        place = place.astype(jnp.int32)

        starts = doc_starts(segments[None])
        places = jnp.arange(n_ctx * rows, dtype=jnp.int32) - starts[0]
        first_head = ctx * wide
        first_block = jnp.zeros((1,), jnp.int32)

        def sum_stats(stats):
            return lax.psum(stats, ("ctx", "tp"))

        ready = (sent,)
    else:
        heads = att // HD
        wide = att
        weight = gather(query_weight, key_weight, value_weight)
        raw = product(both(inner_tokens), weight)
        ready = ()
        squares = jnp.stack(
            [jnp.sum(jnp.square(raw[:, c * wide : (c + 1) * wide]), axis=-1) for c in range(2)]
        )
        place = jnp.arange(2 * rows // math.gcd(rows, 384), dtype=jnp.int32)
        starts = doc_starts(both(segments[None]))
        here = lax.dynamic_slice_in_dim(starts, ctx * rows, rows, axis=1)
        places = (ctx * rows + jnp.arange(rows, dtype=jnp.int32)[None, :] - here).reshape(-1)
        first_head = core * wide
        first_block = ctx.astype(jnp.int32)[None]

        def sum_stats(stats):
            split = stats.reshape(2, 2, rows)
            ordered = jnp.where(core == 0, split, split[:, ::-1])
            total = lax.psum(ordered, ("core", "tp"))
            return jnp.where(core == 0, total, total[:, ::-1]).reshape(stats.shape)

    gate_up_all = gather(gate_weight, up_weight, after=ready)
    down_all = gather(down_weight.T, after=ready)

    my_gains = jnp.stack(
        [
            lax.dynamic_slice_in_dim(query_gain, first_head, wide),
            lax.dynamic_slice_in_dim(key_gain, first_head, wide),
        ]
    )[:, None, :]
    cosine, sine = angles(places)
    edges = starts.reshape(starts.shape[0], n_ctx, rows)
    edges = (edges[:, :, 0], edges[:, :, -1])
    scales = lax.rsqrt(sum_stats(squares) / width + EPSILON)[:, :, None]
    turned = turn(place, raw, scales, my_gains, cosine, sine, heads)
    if by_sequence:
        keys, values = (turned, heads), (turned, 2 * heads)
    else:

        def whole_sequences(columns):
            line = lax.all_gather(columns.reshape(2, rows, wide), "ctx", axis=1, tiled=True)
            return line.reshape(-1, wide)

        keys = (whole_sequences(turned[:, wide : 2 * wide]), 0)
        values = (whole_sequences(turned[:, 2 * wide :]), 0)
    out_att, lse = attend(
        first_block, starts, edges, heads, rows, (turned, 0), keys, values
    )
    if by_sequence:
        received = []
        for step in range(n_ctx):
            start = lax.rem(ctx + step, n_ctx) * rows
            block = lax.dynamic_slice_in_dim(out_att, start, rows)
            received.append(shift_ctx(block, step, n_ctx) if step else block)
        twice = jnp.concatenate(received[::-1] + received[::-1], axis=1)
        own = lax.dynamic_slice_in_dim(twice, (n_ctx - 1 - ctx) * wide, local, axis=1)
        other = swap(lax.dynamic_slice_in_dim(own, (1 - core) * att, att, axis=1), "core")
        attended = jnp.concatenate([lax.dynamic_slice_in_dim(own, core * att, att, axis=1), other])
    else:
        attended = out_att

    spans = [slice(0, short), slice(short, rows)]
    attended = [chunk(attended, j) for j in range(2)]
    parts = [contract_cols(rows_part, out_all).astype(bf16) for rows_part in attended]
    attn_sums = [open_sum(part) for part in parts]

    def forward(j, attn_rows):
        attn_scale = lax.rsqrt(jnp.mean(attn_rows * attn_rows, axis=-1, keepdims=True) + EPSILON)
        attn_unit = attn_rows * attn_scale
        hidden_rows = inner_tokens[spans[j]].astype(f32) + attn_unit * attn_gain
        hidden_low = both(hidden_rows.astype(bf16))
        gate_rows, up_rows, act_low = feed(hidden_low, gate_up_all)
        part = project(act_low, down_all)
        return part, act_low, hidden_low, hidden_rows, attn_scale, attn_unit, gate_rows, up_rows

    def turn_norm(j, state, mlp_rows):
        hidden_rows = state[3]
        mlp_scale = lax.rsqrt(jnp.mean(mlp_rows * mlp_rows, axis=-1, keepdims=True) + EPSILON)
        mlp_unit = mlp_rows * mlp_scale
        output = (hidden_rows + mlp_unit * mlp_gain).astype(bf16)
        grad_out = inner_cotangent[spans[j]].astype(f32)
        gain_part = jnp.sum(grad_out * mlp_unit, axis=0)
        scaled_out = grad_out * mlp_gain
        inner_out = jnp.mean(scaled_out * mlp_unit, axis=-1, keepdims=True)
        grad_mlp_low = both((mlp_scale * (scaled_out - mlp_unit * inner_out)).astype(bf16))
        return grad_mlp_low, output, gain_part

    def turn_back(state, grad_mlp_low):
        gate_rows, up_rows = state[6:]
        grad_gate_low, grad_up_low = feed_back(grad_mlp_low, down_all, gate_rows, up_rows)
        back = project_both(grad_gate_low, grad_up_low, gate_up_all)
        return back, grad_gate_low, grad_up_low

    def close_back(j, state, back_rows):
        attn_scale, attn_unit = state[4], state[5]
        grad_hidden = inner_cotangent[spans[j]].astype(f32) + back_rows
        gain_part = jnp.sum(grad_hidden * attn_unit, axis=0)
        scaled_hidden = grad_hidden * attn_gain
        inner_hidden = jnp.mean(scaled_hidden * attn_unit, axis=-1, keepdims=True)
        grad_attn_low = both((attn_scale * (scaled_hidden - attn_unit * inner_hidden)).astype(bf16))
        grad_att = product(grad_attn_low, out_all).astype(bf16)
        return grad_att, grad_attn_low, grad_hidden, gain_part

    fore_a = forward(0, close_sum(*attn_sums[0]))
    mlp_a = open_sum(fore_a[0])
    fore_b = forward(1, close_sum(attn_sums[1][0], tie(attn_sums[1][1], fore_a[0])))
    mlp_b = open_sum(fore_b[0])
    norm_a = turn_norm(0, fore_a, close_sum(mlp_a[0], tie(mlp_a[1], fore_b[0])))
    back_a = turn_back(fore_a, norm_a[0])
    hid_a = open_sum(back_a[0])
    norm_b = turn_norm(1, fore_b, close_sum(mlp_b[0], tie(mlp_b[1], back_a[0])))
    down_grad = outer((norm_a[0], norm_b[0]), (fore_a[1], fore_b[1]))
    down_low = scatter(down_grad)
    back_b = turn_back(fore_b, tie(norm_b[0], down_grad))
    hid_b = open_sum(back_b[0])
    hiddens = (fore_a[2], fore_b[2])
    close_a = close_back(0, fore_a, close_sum(hid_a[0], tie(hid_a[1], back_b[0])))
    gate_grad = outer(hiddens, (back_a[1], back_b[1]))
    gate_low = scatter(gate_grad)
    close_b = close_back(1, fore_b, close_sum(hid_b[0], tie(hid_b[1], gate_grad)))
    up_low = scatter(outer(hiddens, (back_a[2], back_b[2])))
    out_theirs, out_mine = (
        outer(
            [
                lax.dynamic_slice_in_dim(close[1], index * half, half, axis=1)
                for close in (close_a, close_b)
            ],
            attended,
        )
        for index in (1 - here_y, here_y)
    )
    out_total = (out_mine.astype(f32) + swap(out_theirs, "y").astype(f32)).astype(bf16)
    out_sent = []
    for step in range(n_ctx):
        start = lax.rem(ctx + step, n_ctx) * 2 * piece
        block = lax.dynamic_slice_in_dim(out_total, start, 2 * piece)
        out_sent.append(shift_ctx(block, step, n_ctx) if step else block)
    out_low = sum(block.astype(f32) for block in out_sent).astype(bf16)
    grad_att = unchunk([close_a[0], close_b[0]])

    if by_sequence:
        own = beside(core, grad_att[:rows], swap(grad_att[rows:], "core"))
        received = []
        for step in range(n_ctx):
            start = lax.rem(ctx + step, n_ctx) * wide
            block = lax.dynamic_slice_in_dim(own, start, wide, axis=1)
            received.append(shift_ctx(block, step, n_ctx) if step else block)
        grad_att = by_source(received, ctx).reshape(n_ctx * rows, wide)
    dq, dk, dv = attend_back(
        first_block, starts, edges, heads, rows, lse, (turned, 0), out_att, grad_att, keys, values
    )
    if not by_sequence:

        def own_rows(grads):
            split = grads.reshape(2, n_ctx * rows, wide)
            low = lax.psum_scatter(split, "ctx", scatter_dimension=1, tiled=True)
            return low.reshape(2 * rows, wide)

        dk, dv = own_rows(dk), own_rows(dv)
    scaled, inner, gain_sums = unturn(
        place, dq, dk, raw, scales, my_gains, cosine, sine, heads
    )
    inner = sum_stats(inner[:, :, 0])[:, :, None] / width
    grad_qkv = norm_back(place, scaled, raw, scales, inner, dv, heads)

    if by_sequence:
        weight_halves = weight.reshape(2, half, 3 * wide)
        weight_mine = lax.dynamic_index_in_dim(weight_halves, here_x, 0, keepdims=False)
        weight_theirs = lax.dynamic_index_in_dim(weight_halves, 1 - here_x, 0, keepdims=False)
        grad_blocks = [grad_qkv[step * rows : (step + 1) * rows] for step in range(n_ctx)]
        others = [
            swap(contract_cols(block, weight_theirs).astype(bf16), "tp") for block in grad_blocks
        ]

        def y_half(index, after):
            tied = tie(grad_qkv, after)
            return sum(
                contract_rows(
                    lax.dynamic_slice_in_dim(block, index * half, half, axis=1),
                    tied[step * rows : (step + 1) * rows],
                )
                for step, block in enumerate(blocks)
            )

        terms = []
        for step in range(n_ctx):
            block = grad_blocks[step]
            if step == n_ctx - 1:
                block = tie(block, qkv_theirs)
            term = contract_cols(block, weight_mine) + others[step].astype(f32)
            if step < n_ctx - 1:
                low = term.astype(bf16)
                if step == 1:
                    qkv_theirs = y_half(1 - here_y, low).astype(bf16)
                term = shift_ctx(low, -1 - step, n_ctx).astype(f32)
            terms.append(term)
        dx = lowered(sum(terms))
        dx_rows = beside(here_x, dx, swap(dx, "tp")).astype(f32)

        qkv_total = y_half(here_y, qkv_theirs) + swap(qkv_theirs, "y").astype(f32)
        split = qkv_total.reshape(2, n_ctx * piece, 3 * wide)
        mine = lax.dynamic_index_in_dim(split, core, 0, keepdims=False)
        qkv_low = lax.dynamic_index_in_dim(split, 1 - core, 0, keepdims=False)
        qkv_low = (mine + swap(qkv_low.astype(bf16), "core").astype(f32)).astype(bf16)
        received = []
        for step in range(n_ctx):
            start = lax.rem(ctx + step, n_ctx) * piece
            block = lax.dynamic_slice_in_dim(qkv_low, start, piece)
            received.append(shift_ctx(block, step, n_ctx) if step else block)
        lines = by_source(received, ctx)
        qkv_shards = [
            jnp.concatenate([lines[n, :, c * wide : (c + 1) * wide] for n in range(n_ctx)], axis=1)
            .astype(f32)
            for c in range(3)
        ]
    else:
        grad_rows = [chunk(grad_qkv, j) for j in range(2)]
        token_rows = both(inner_tokens)
        token_rows = [chunk(token_rows, j) for j in range(2)]
        qkv_shards = [
            own_share(scatter(outer(token_rows, [r[:, c * wide : (c + 1) * wide] for r in grad_rows])))
            for c in range(3)
        ]
        sums = [open_sum(contract_cols(rows_part, weight).astype(bf16)) for rows_part in grad_rows]
        dx_rows = reorder(jnp.concatenate([close_sum(*parts) for parts in sums]), outward)
    grad_tokens = reorder(jnp.concatenate([close_a[2], close_b[2]]), outward) + dx_rows

    spread = jnp.zeros((2, local), f32)
    spread = lax.dynamic_update_slice(spread, gain_sums[:, 0], (jnp.int32(0), first_head))
    gains = jnp.concatenate([spread.reshape(-1), close_a[3] + close_b[3], norm_a[2] + norm_b[2]])
    if by_sequence:
        gains, down_low, gate_low, up_low = (
            tie(values, dx) for values in (gains, down_low, gate_low, up_low)
        )
    gains = lax.psum(gains, ("y", "core", "ctx"))
    cuts = [local, 2 * local, 2 * local + width]
    query_gain_grad, key_gain_grad, attn_gain_grad, mlp_gain_grad = jnp.split(gains, cuts)
    attn_gain_grad, mlp_gain_grad = (
        jnp.concatenate([gain[n * piece : (n + 1) * piece] for n in outward])
        for gain in (attn_gain_grad, mlp_gain_grad)
    )
    return (
        reorder(jnp.concatenate([norm_a[1], norm_b[1]]), outward),
        grad_tokens,
        *qkv_shards,
        own_share(out_low).T,
        own_share(gate_low),
        own_share(up_low),
        own_share(down_low).T,
        query_gain_grad,
        key_gain_grad,
        attn_gain_grad,
        mlp_gain_grad,
    )


def solution(mesh):
    sizes = {"y": mesh.shape["dp"] // 2, "core": 2, "ctx": mesh.shape["ctx"], "tp": mesh.shape["tp"]}
    split = Mesh(mesh.devices.reshape(tuple(sizes.values())), tuple(sizes))
    dp = ("y", "core")
    every = ("y", "core", "ctx")
    in_specs = (
        P(every, None),
        P(dp),
        P(every, "tp"),
        P(every, "tp"),
        P(every, "tp"),
        P("tp", every),
        P(every, "tp"),
        P(every, "tp"),
        P("tp", every),
        P("tp"),
        P("tp"),
        P(),
        P(),
        P(every, None),
    )
    out_specs = (
        P(every, None),
        P(every, None),
        P(every, "tp"),
        P(every, "tp"),
        P(every, "tp"),
        P("tp", every),
        P(every, "tp"),
        P(every, "tp"),
        P("tp", every),
        P("tp"),
        P("tp"),
        P(),
        P(),
    )
    return jax.shard_map(
        functools.partial(body, sizes=sizes),
        mesh=split,
        in_specs=in_specs,
        out_specs=out_specs,
        check_vma=False,
    )
```

```python
import functools
import math

import jax
import jax.numpy as jnp
from jax import lax
from jax.experimental import pallas as pl
from jax.experimental.pallas import tpu as pltpu
from jax.sharding import Mesh
from jax.sharding import PartitionSpec as P

HD = 128
EPSILON = 1e-06
ROPE_BASE = 500000.0
MASKED = -1e30
SCALING = HD**-0.5
LOG2E = math.log2(math.e)
BLOCK_K = 256
VMEM_LIMIT = 48 << 20
bf16 = jnp.bfloat16
f32 = jnp.float32


def cost(products, moved):
    return pl.CostEstimate(flops=products, bytes_accessed=moved // 2, transcendentals=0)


def dims(left, right, over):
    return lax.dot_general(left, right, (over, ((), ())), preferred_element_type=f32)


def product(left, right):
    return dims(left, right, ((1,), (0,)))


def contract_rows(left, right):
    return dims(left, right, ((0,), (0,)))


def contract_cols(left, right):
    return dims(left, right, ((1,), (1,)))


def key_steps(block, low, high, bk, per_block):
    end = block * per_block
    begin = jnp.minimum(low // bk, end)
    clear = jnp.minimum((high + bk - 1) // bk, end)
    return begin, clear, end


def diagonal(step, scores, start, first, bk):
    key = step * bk + lax.broadcasted_iota(jnp.int32, scores.shape, 0)
    place = step * bk + lax.broadcasted_iota(jnp.int32, scores.shape, 1)
    return jnp.where((key <= place) & (key + first >= start), scores, MASKED)


def attend_kernel(
    first_ref, low_ref, high_ref, start_ref, q_ref, k_ref, v_ref, o_ref, lse_ref, *, bk
):
    size = q_ref.shape[0]
    per_block = size // bk
    block = first_ref[0] + pl.program_id(2)
    sequence = pl.program_id(1)
    queries = q_ref[...]
    start = start_ref[0]

    def update(carry, scores, values):
        peak, total, acc = carry
        new_peak = jnp.maximum(peak, jnp.max(scores, axis=0, keepdims=True))
        weights = jnp.exp2(scores - new_peak)
        shrink = jnp.exp2(peak - new_peak)
        total = total * shrink + jnp.sum(weights, axis=0, keepdims=True)
        acc = acc * shrink + contract_rows(values, weights.astype(bf16))
        return new_peak, total, acc

    def clear_step(j, carry):
        rows = pl.ds(pl.multiple_of(j * bk, bk), bk)
        return update(carry, contract_cols(k_ref[rows, :], queries), v_ref[rows, :])

    def masked_step(j, carry):
        rows = pl.ds(pl.multiple_of(j * bk, bk), bk)
        scores = contract_cols(k_ref[rows, :], queries)
        key = j * bk + lax.broadcasted_iota(jnp.int32, (bk, 1), 0)
        return update(carry, jnp.where(key >= start, scores, MASKED), v_ref[rows, :])

    begin, clear, end = key_steps(
        block, low_ref[sequence, block], high_ref[sequence, block], bk, per_block
    )
    carry = (
        jnp.full((1, size), MASKED, f32),
        jnp.zeros((1, size), f32),
        jnp.zeros((HD, size), f32),
    )
    carry = lax.fori_loop(begin, clear, masked_step, carry)
    carry = lax.fori_loop(jnp.maximum(begin, clear), end, clear_step, carry)
    for step in range(per_block):
        cut = step * bk
        rows = pl.ds(pl.multiple_of(block * size + cut, bk), bk)
        scores = contract_cols(k_ref[rows, :], queries[cut:])
        scores = diagonal(step, scores, start[:, cut:], block * size, bk)
        right = update(tuple(part[:, cut:] for part in carry), scores, v_ref[rows, :])
        if cut:
            right = tuple(
                jnp.concatenate([part[:, :cut], new], axis=1) for part, new in zip(carry, right)
            )
        carry = right
    peak, total, acc = carry
    o_ref[...] = (acc / total).T.astype(bf16)
    lse_ref[0] = peak + jnp.log2(total)


def attend(first, starts, edges, heads, size, query, key, value):
    sequences, length = starts.shape
    slots = query[0].shape[0] // (sequences * size)
    rows = query[0].shape[0]

    def part(offset):
        return pl.BlockSpec((size, HD), lambda g, b, s, *refs: (b * slots + s, offset + g))

    def whole(offset):
        return pl.BlockSpec((length, HD), lambda g, b, s, *refs: (b, offset + g))

    return pl.pallas_call(
        functools.partial(attend_kernel, bk=min(BLOCK_K, size)),
        grid_spec=pltpu.PrefetchScalarGridSpec(
            num_scalar_prefetch=3,
            grid=(heads, sequences, slots),
            in_specs=[
                pl.BlockSpec((1, 1, size), lambda g, b, s, first, *refs: (b, 0, first[0] + s)),
                part(query[1]),
                whole(key[1]),
                whole(value[1]),
            ],
            out_specs=[
                part(0),
                pl.BlockSpec((1, 1, size), lambda g, b, s, *refs: (g, 0, b * slots + s)),
            ],
        ),
        out_shape=[
            jax.ShapeDtypeStruct((rows, heads * HD), bf16),
            jax.ShapeDtypeStruct((heads, 1, rows), f32),
        ],
        cost_estimate=cost(4 * HD * heads * rows * length, 0),
        compiler_params=pltpu.CompilerParams(vmem_limit_bytes=VMEM_LIMIT),
        name="attend",
    )(first, *edges, starts[:, None, :], query[0], key[0], value[0])


def attend_back_kernel(
    first_ref,
    low_ref,
    high_ref,
    start_ref,
    lse_ref,
    q_ref,
    o_ref,
    do_ref,
    k_ref,
    v_ref,
    dq_ref,
    dk_ref,
    dv_ref,
    dk_sum,
    dv_sum,
    *,
    bk,
):
    size = q_ref.shape[0]
    per_block = size // bk
    block = first_ref[0] + pl.program_id(2)
    sequence = pl.program_id(1)
    queries = q_ref[...]
    grads = do_ref[...]
    start = start_ref[0]
    lse = lse_ref[0]
    delta = jnp.sum((grads.astype(f32) * o_ref[...].astype(f32)).T, axis=0, keepdims=True)

    @pl.when(pl.program_id(2) == 0)
    def _():
        dk_sum[...] = jnp.zeros_like(dk_sum)
        dv_sum[...] = jnp.zeros_like(dv_sum)

    def update(dq, scores, rows, cut):
        probs = jnp.exp2(scores - lse[:, cut:])
        dv_sum[rows, :] += product(probs.astype(bf16), grads[cut:])
        dprobs = contract_cols(v_ref[rows, :], grads[cut:])
        dscores = (probs * (dprobs - delta[:, cut:])).astype(bf16)
        dk_sum[rows, :] += product(dscores, queries[cut:])
        return dq + contract_rows(k_ref[rows, :], dscores)

    def clear_step(j, dq):
        rows = pl.ds(pl.multiple_of(j * bk, bk), bk)
        return update(dq, contract_cols(k_ref[rows, :], queries), rows, 0)

    def masked_step(j, dq):
        rows = pl.ds(pl.multiple_of(j * bk, bk), bk)
        scores = contract_cols(k_ref[rows, :], queries)
        key = j * bk + lax.broadcasted_iota(jnp.int32, (bk, 1), 0)
        return update(dq, jnp.where(key >= start, scores, MASKED), rows, 0)

    begin, clear, end = key_steps(
        block, low_ref[sequence, block], high_ref[sequence, block], bk, per_block
    )
    dq = jnp.zeros((HD, size), f32)
    dq = lax.fori_loop(begin, clear, masked_step, dq)
    dq = lax.fori_loop(jnp.maximum(begin, clear), end, clear_step, dq)
    for step in range(per_block):
        cut = step * bk
        rows = pl.ds(pl.multiple_of(block * size + cut, bk), bk)
        scores = contract_cols(k_ref[rows, :], queries[cut:])
        scores = diagonal(step, scores, start[:, cut:], block * size, bk)
        right = update(dq[:, cut:], scores, rows, cut)
        dq = jnp.concatenate([dq[:, :cut], right], axis=1) if cut else right
    dq_ref[...] = (dq.T * SCALING).astype(bf16)

    @pl.when(pl.program_id(2) == pl.num_programs(2) - 1)
    def _():
        dk_ref[...] = (dk_sum[...] * (1.0 / LOG2E)).astype(bf16)
        dv_ref[...] = dv_sum[...].astype(bf16)


def attend_back(first, starts, edges, heads, size, lse, query, out, grad, key, value):
    sequences, length = starts.shape
    rows = query[0].shape[0]
    slots = rows // (sequences * size)

    def part(offset):
        return pl.BlockSpec((size, HD), lambda g, b, s, *refs: (b * slots + s, offset + g))

    def whole(offset):
        return pl.BlockSpec((length, HD), lambda g, b, s, *refs: (b, offset + g))

    return pl.pallas_call(
        functools.partial(attend_back_kernel, bk=min(BLOCK_K, size)),
        grid_spec=pltpu.PrefetchScalarGridSpec(
            num_scalar_prefetch=3,
            grid=(heads, sequences, slots),
            in_specs=[
                pl.BlockSpec((1, 1, size), lambda g, b, s, first, *refs: (b, 0, first[0] + s)),
                pl.BlockSpec((1, 1, size), lambda g, b, s, *refs: (g, 0, b * slots + s)),
                part(query[1]),
                part(0),
                part(0),
                whole(key[1]),
                whole(value[1]),
            ],
            out_specs=[part(0), whole(0), whole(0)],
            scratch_shapes=[pltpu.VMEM((length, HD), f32)] * 2,
        ),
        out_shape=[
            jax.ShapeDtypeStruct((rows, heads * HD), bf16),
            jax.ShapeDtypeStruct((sequences * length, heads * HD), bf16),
            jax.ShapeDtypeStruct((sequences * length, heads * HD), bf16),
        ],
        cost_estimate=cost(5 * HD * heads * rows * length, 0),
        compiler_params=pltpu.CompilerParams(vmem_limit_bytes=VMEM_LIMIT),
        name="attend_back",
    )(first, *edges, starts[:, None, :], lse, query[0], out, grad, key[0], value[0])


def turn_kernel(place_ref, raw_ref, scale_ref, gain_ref, cos_ref, sin_ref, out_ref, *, heads):
    for c in range(3):
        for h in range(heads):
            cols = slice((c * heads + h) * HD, (c * heads + h + 1) * HD)
            values = raw_ref[:, cols]
            if c < 2:
                values = values * scale_ref[c] * gain_ref[c, :, h * HD : (h + 1) * HD]
                values = values * cos_ref[...] + pltpu.roll(values, HD // 2, 1) * sin_ref[...]
            if c == 0:
                values = values * (SCALING * LOG2E)
            out_ref[:, cols] = values.astype(bf16)


def turn(place, raw, scales, gains, cosine, sine, heads):
    rows = raw.shape[0]
    size = rows // place.shape[0]
    return pl.pallas_call(
        functools.partial(turn_kernel, heads=heads),
        grid_spec=pltpu.PrefetchScalarGridSpec(
            num_scalar_prefetch=1,
            grid=(rows // size,),
            in_specs=[
                pl.BlockSpec((size, 3 * heads * HD), lambda i, place: (place[i], 0)),
                pl.BlockSpec((2, size, 1), lambda i, place: (0, i, 0)),
                pl.BlockSpec((2, 1, heads * HD), lambda i, place: (0, 0, 0)),
                pl.BlockSpec((size, HD), lambda i, place: (i, 0)),
                pl.BlockSpec((size, HD), lambda i, place: (i, 0)),
            ],
            out_specs=pl.BlockSpec((size, 3 * heads * HD), lambda i, place: (i, 0)),
        ),
        out_shape=jax.ShapeDtypeStruct(raw.shape, bf16),
        cost_estimate=cost(0, 20 * rows * heads * HD),
        compiler_params=pltpu.CompilerParams(vmem_limit_bytes=VMEM_LIMIT),
        name="turn",
    )(place, raw, scales, gains, cosine, sine)


def unturn_kernel(
    place_ref,
    dq_ref,
    dk_ref,
    raw_ref,
    scale_ref,
    gain_ref,
    cos_ref,
    sin_ref,
    out_ref,
    inner_ref,
    sum_ref,
    *,
    heads,
):
    @pl.when(pl.program_id(0) == 0)
    def _():
        sum_ref[...] = jnp.zeros_like(sum_ref)

    for c, grad_ref in enumerate((dq_ref, dk_ref)):
        inner = 0.0
        for h in range(heads):
            head = slice(h * HD, (h + 1) * HD)
            cols = slice((c * heads + h) * HD, (c * heads + h + 1) * HD)
            grad = grad_ref[:, head].astype(f32)
            normed = grad * cos_ref[...] - pltpu.roll(grad, HD // 2, 1) * sin_ref[...]
            unit = raw_ref[:, cols] * scale_ref[c]
            scaled = normed * gain_ref[c, :, head]
            out_ref[:, cols] = scaled
            inner = inner + jnp.sum(scaled * unit, axis=1, keepdims=True)
            sum_ref[c, :, head] += jnp.sum(normed * unit, axis=0, keepdims=True)
        inner_ref[c] = inner


def unturn(place, dq, dk, raw, scales, gains, cosine, sine, heads):
    rows = raw.shape[0]
    size = rows // place.shape[0]
    width = heads * HD
    return pl.pallas_call(
        functools.partial(unturn_kernel, heads=heads),
        grid_spec=pltpu.PrefetchScalarGridSpec(
            num_scalar_prefetch=1,
            grid=(rows // size,),
            in_specs=[
                pl.BlockSpec((size, width), lambda i, place: (i, 0)),
                pl.BlockSpec((size, width), lambda i, place: (i, 0)),
                pl.BlockSpec((size, 3 * width), lambda i, place: (place[i], 0)),
                pl.BlockSpec((2, size, 1), lambda i, place: (0, i, 0)),
                pl.BlockSpec((2, 1, width), lambda i, place: (0, 0, 0)),
                pl.BlockSpec((size, HD), lambda i, place: (i, 0)),
                pl.BlockSpec((size, HD), lambda i, place: (i, 0)),
            ],
            out_specs=[
                pl.BlockSpec((size, 2 * width), lambda i, place: (i, 0)),
                pl.BlockSpec((2, size, 1), lambda i, place: (0, i, 0)),
                pl.BlockSpec((2, 1, width), lambda i, place: (0, 0, 0)),
            ],
        ),
        out_shape=[
            jax.ShapeDtypeStruct((rows, 2 * width), f32),
            jax.ShapeDtypeStruct((2, rows, 1), f32),
            jax.ShapeDtypeStruct((2, 1, width), f32),
        ],
        cost_estimate=cost(0, 32 * rows * width),
        compiler_params=pltpu.CompilerParams(vmem_limit_bytes=VMEM_LIMIT),
        name="unturn",
    )(place, dq, dk, raw, scales, gains, cosine, sine)


def norm_back_kernel(
    place_ref, scaled_ref, raw_ref, scale_ref, inner_ref, dv_ref, out_ref, *, heads
):
    width = heads * HD
    for c in range(2):
        cols = slice(c * width, (c + 1) * width)
        unit = raw_ref[:, cols] * scale_ref[c]
        out_ref[:, cols] = (scale_ref[c] * (scaled_ref[:, cols] - unit * inner_ref[c])).astype(bf16)
    out_ref[:, 2 * width :] = dv_ref[...]


def norm_back(place, scaled, raw, scales, inner, dv, heads):
    rows = raw.shape[0]
    size = rows // place.shape[0]
    width = heads * HD
    return pl.pallas_call(
        functools.partial(norm_back_kernel, heads=heads),
        grid_spec=pltpu.PrefetchScalarGridSpec(
            num_scalar_prefetch=1,
            grid=(rows // size,),
            in_specs=[
                pl.BlockSpec((size, 2 * width), lambda i, place: (i, 0)),
                pl.BlockSpec((size, 3 * width), lambda i, place: (place[i], 0)),
                pl.BlockSpec((2, size, 1), lambda i, place: (0, i, 0)),
                pl.BlockSpec((2, size, 1), lambda i, place: (0, i, 0)),
                pl.BlockSpec((size, width), lambda i, place: (i, 0)),
            ],
            out_specs=pl.BlockSpec((size, 3 * width), lambda i, place: (place[i], 0)),
        ),
        out_shape=jax.ShapeDtypeStruct((rows, 3 * width), bf16),
        cost_estimate=cost(0, 24 * rows * width),
        compiler_params=pltpu.CompilerParams(vmem_limit_bytes=VMEM_LIMIT),
        name="norm_back",
    )(place, scaled, raw, scales, inner, dv)


def reorder_kernel(in_ref, out_ref, *, order):
    size = in_ref.shape[1] // len(order)
    for n, m in enumerate(order):
        out_ref[:, n * size : (n + 1) * size] = in_ref[:, m * size : (m + 1) * size]


def reorder(values, order):
    rows, width = values.shape
    size = math.gcd(rows, 192)
    spec = pl.BlockSpec((size, width), lambda i: (i, 0))
    return pl.pallas_call(
        functools.partial(reorder_kernel, order=order),
        grid=(rows // size,),
        in_specs=[spec],
        out_specs=spec,
        out_shape=jax.ShapeDtypeStruct(values.shape, values.dtype),
        cost_estimate=cost(0, 2 * values.size * values.dtype.itemsize),
        compiler_params=pltpu.CompilerParams(vmem_limit_bytes=VMEM_LIMIT),
        name="reorder",
    )(values)


def outer_kernel(left_a, left_b, right_a, right_b, out_ref):
    total = contract_rows(left_a[...], right_a[...]) + contract_rows(left_b[...], right_b[...])
    out_ref[...] = total.astype(bf16)


def outer(lefts, rights):
    rows, high = lefts[0].shape
    wide = rights[0].shape[1]
    tall, broad = math.gcd(high, 512), math.gcd(wide, 1024)
    left = pl.BlockSpec((rows, tall), lambda i, j: (0, i))
    right = pl.BlockSpec((rows, broad), lambda i, j: (0, j))
    return pl.pallas_call(
        outer_kernel,
        grid=(high // tall, wide // broad),
        in_specs=[left, left, right, right],
        out_specs=pl.BlockSpec((tall, broad), lambda i, j: (i, j)),
        out_shape=jax.ShapeDtypeStruct((high, wide), bf16),
        cost_estimate=cost(2 * rows * high * wide, 0),
        compiler_params=pltpu.CompilerParams(vmem_limit_bytes=VMEM_LIMIT),
        name="outer",
    )(*lefts, *rights)


def feed_kernel(hidden_ref, gate_ref, up_ref, gate_out, up_out, act_out):
    gate = product(hidden_ref[...], gate_ref[...])
    up = product(hidden_ref[...], up_ref[...])
    gate_out[...] = gate.astype(bf16)
    up_out[...] = up.astype(bf16)
    act_out[...] = (gate * jax.nn.sigmoid(gate) * up).astype(bf16)


def feed(hidden, gate, up_down):
    rows, width = hidden.shape
    units = gate.shape[1]
    wide = math.gcd(units, 512)
    out = pl.BlockSpec((rows, wide), lambda j: (0, j))
    return pl.pallas_call(
        feed_kernel,
        grid=(units // wide,),
        in_specs=[
            pl.BlockSpec((rows, width), lambda j: (0, 0)),
            pl.BlockSpec((width, wide), lambda j: (0, j)),
            pl.BlockSpec((width, wide), lambda j: (0, j)),
        ],
        out_specs=[out, out, out],
        out_shape=[jax.ShapeDtypeStruct((rows, units), bf16)] * 3,
        cost_estimate=cost(2 * rows * width * units, 0),
        compiler_params=pltpu.CompilerParams(vmem_limit_bytes=VMEM_LIMIT),
        name="feed",
    )(hidden, gate, up_down)


def project_kernel(left_ref, right_ref, out_ref):
    out_ref[...] = contract_cols(left_ref[...], right_ref[...]).astype(bf16)


def project(act, up_down):
    rows, units = act.shape
    width = up_down.shape[0]
    wide = math.gcd(width, 512)
    return pl.pallas_call(
        project_kernel,
        grid=(width // wide,),
        in_specs=[
            pl.BlockSpec((rows, units), lambda j: (0, 0)),
            pl.BlockSpec((wide, units), lambda j: (j, 1)),
        ],
        out_specs=pl.BlockSpec((rows, wide), lambda j: (0, j)),
        out_shape=jax.ShapeDtypeStruct((rows, width), bf16),
        cost_estimate=cost(rows * units * width, 0),
        compiler_params=pltpu.CompilerParams(vmem_limit_bytes=VMEM_LIMIT),
        name="project",
    )(act, up_down)


def feed_back_kernel(grad_ref, down_ref, gate_ref, up_ref, gate_out, up_out):
    grad = product(grad_ref[...], down_ref[...])
    gate = gate_ref[...].astype(f32)
    sigmoid = jax.nn.sigmoid(gate)
    gate_out[...] = (
        grad * up_ref[...].astype(f32) * (sigmoid * (1.0 + gate * (1.0 - sigmoid)))
    ).astype(bf16)
    up_out[...] = (grad * (gate * sigmoid)).astype(bf16)


def feed_back(grad, up_down, gate, up):
    rows, width = grad.shape
    units = gate.shape[1]
    wide = math.gcd(units, 512)
    count = units // wide
    part = pl.BlockSpec((rows, wide), lambda j: (0, j))
    return pl.pallas_call(
        feed_back_kernel,
        grid=(count,),
        in_specs=[
            pl.BlockSpec((rows, width), lambda j: (0, 0)),
            pl.BlockSpec((width, wide), lambda j: (0, count + j)),
            part,
            part,
        ],
        out_specs=[part, part],
        out_shape=[jax.ShapeDtypeStruct((rows, units), bf16)] * 2,
        cost_estimate=cost(rows * width * units, 0),
        compiler_params=pltpu.CompilerParams(vmem_limit_bytes=VMEM_LIMIT),
        name="feed_back",
    )(grad, up_down, gate, up)


def project_both_kernel(gate_grad, up_grad, gate_ref, up_ref, out_ref):
    total = contract_cols(gate_grad[...], gate_ref[...]) + contract_cols(up_grad[...], up_ref[...])
    out_ref[...] = total.astype(bf16)


def project_both(gate_grad, up_grad, gate, up_down):
    rows, units = gate_grad.shape
    width = gate.shape[0]
    wide = math.gcd(width, 512)
    left = pl.BlockSpec((rows, units), lambda j: (0, 0))
    return pl.pallas_call(
        project_both_kernel,
        grid=(width // wide,),
        in_specs=[
            left,
            left,
            pl.BlockSpec((wide, units), lambda j: (j, 0)),
            pl.BlockSpec((wide, units), lambda j: (j, 0)),
        ],
        out_specs=pl.BlockSpec((rows, wide), lambda j: (0, j)),
        out_shape=jax.ShapeDtypeStruct((rows, width), bf16),
        cost_estimate=cost(2 * rows * units * width, 0),
        compiler_params=pltpu.CompilerParams(vmem_limit_bytes=VMEM_LIMIT),
        name="project_both",
    )(gate_grad, up_grad, gate, up_down)


def tie_kernel(*refs):
    pass


def tie(values, *others):
    return pl.pallas_call(
        tie_kernel,
        in_specs=[pl.BlockSpec(memory_space=pl.ANY)] * (1 + len(others)),
        out_specs=pl.BlockSpec(memory_space=pl.ANY),
        out_shape=jax.ShapeDtypeStruct(values.shape, values.dtype),
        input_output_aliases={0: 0},
        cost_estimate=cost(0, 0),
        name="tie",
    )(values, *others)


def doc_starts(doc_ids):
    row_index = jnp.arange(doc_ids.shape[-1], dtype=jnp.int32)
    is_start = jnp.concatenate(
        [jnp.ones_like(doc_ids[:, :1], dtype=bool), doc_ids[:, 1:] != doc_ids[:, :-1]], axis=1
    )
    return lax.cummax(jnp.where(is_start, row_index[None, :], 0), axis=1)


def angles(places):
    frequency = ROPE_BASE ** (-(jnp.arange(HD // 2, dtype=f32) * 2.0 / HD))
    phases = places.astype(f32)[:, None] * frequency[None, :]
    cosine, sine = jnp.cos(phases), jnp.sin(phases)
    return (
        jnp.concatenate([cosine, cosine], axis=-1),
        jnp.concatenate([-sine, sine], axis=-1),
    )


def swap(values, axis):
    return lax.ppermute(values, axis, [(0, 1), (1, 0)])


def shift_ctx(values, steps, size):
    return lax.ppermute(values, "ctx", [(i, (i + steps) % size) for i in range(size)])


def by_source(received, me):
    size = len(received)
    turned = jnp.stack(received[::-1] + received[::-1])
    return lax.dynamic_slice_in_dim(turned, size - 1 - me, size, axis=0)


def in_order(index, mine, theirs):
    return jnp.where(index == 0, jnp.stack([mine, theirs]), jnp.stack([theirs, mine]))


def beside(index, mine, theirs):
    first = jnp.where(index == 0, mine, theirs)
    second = jnp.where(index == 0, theirs, mine)
    return jnp.concatenate([first, second], axis=1)


def lowered(values):
    return lax.reduce_precision(values, 8, 7).astype(bf16)


def body(
    tokens,
    segments,
    query_weight,
    key_weight,
    value_weight,
    out_weight,
    gate_weight,
    up_weight,
    down_weight,
    query_gain,
    key_gain,
    attn_gain,
    mlp_gain,
    cotangent,
    *,
    sizes,
):
    core = lax.axis_index("core")
    ctx = lax.axis_index("ctx")
    here_y = lax.axis_index("y")
    here_x = lax.axis_index("tp")
    n_ctx, n_tp = sizes["ctx"], sizes["tp"]
    rows, width = tokens.shape
    piece = query_weight.shape[0]
    local = query_weight.shape[1]
    att = local // 2
    half = width // 2
    short = rows // 2

    def column_half(values, index):
        size = values.shape[1] // 2
        return lax.dynamic_slice_in_dim(values, index * size, size, axis=1)

    def number(y, c, z):
        return (y * 2 + c) * n_ctx + z

    inward = [number(y, c, z) for y in range(2) for z in range(n_ctx) for c in range(2)]
    outward = [inward.index(n) for n in range(4 * n_ctx)]

    def gather(*shards, after=(), axes=("y", "ctx")):
        mine = jnp.concatenate([column_half(shard, core) for shard in shards], axis=1)
        theirs = jnp.concatenate([column_half(shard, 1 - core) for shard in shards], axis=1)
        pair = in_order(core, mine, swap(theirs, "core")).reshape(2 * piece, -1)
        if after:
            pair = tie(pair, *after)
        return lax.all_gather(pair, axes, axis=0, tiled=True)

    def scatter(grad):
        return lax.psum_scatter(grad, ("y", "ctx"), scatter_dimension=0, tiled=True)

    def own_share(low):
        mine = lax.dynamic_slice_in_dim(low, core * piece, piece)
        theirs = swap(lax.dynamic_slice_in_dim(low, (1 - core) * piece, piece), "core")
        return beside(core, mine, theirs).astype(f32)

    def both(values):
        return jnp.concatenate([values, swap(values, "core")], axis=0)

    def open_sum(part):
        part = part.reshape(2, -1, width)
        total = part[0].astype(f32) + swap(part[1], "core").astype(f32)
        if n_tp == 2:
            low = lowered(total)
            return low, swap(low, "tp")
        low = lax.psum(total.astype(bf16), "tp")
        return low, jnp.zeros_like(low)

    def close_sum(low, other):
        return low.astype(f32) + other.astype(f32)

    def chunk(values, j):
        split = values.reshape(2, rows, -1)[:, j * short : (j + 1) * short]
        return split.reshape(2 * short, -1)

    def unchunk(parts):
        split = [part.reshape(2, short, -1) for part in parts]
        return jnp.concatenate(split, axis=1).reshape(2 * rows, -1)

    by_sequence = n_tp == 2 and (local // HD) % n_ctx == 0
    out_all = gather(out_weight.T)
    inner_tokens = reorder(tokens, inward)
    inner_cotangent = reorder(cotangent, inward)
    attn_gain, mlp_gain = (
        jnp.concatenate([gain[n * piece : (n + 1) * piece] for n in inward])
        for gain in (attn_gain, mlp_gain)
    )

    if by_sequence:
        heads = local // HD // n_ctx
        wide = heads * HD

        def shard_columns(index):
            return jnp.concatenate(
                [
                    lax.dynamic_slice_in_dim(shard, index * wide, wide, axis=1)
                    for shard in (query_weight, key_weight, value_weight)
                ],
                axis=1,
            )

        columns = [shard_columns(ctx)]
        for step in range(1, n_ctx):
            columns.append(shift_ctx(shard_columns(lax.rem(ctx + step, n_ctx)), step, n_ctx))
        weight = by_source(columns, ctx).reshape(n_ctx * piece, 3 * wide)
        weight = in_order(core, weight, swap(weight, "core")).reshape(half, 3 * wide)
        weight = in_order(here_y, weight, swap(weight, "y")).reshape(width, 3 * wide)

        sent = lax.dynamic_slice_in_dim(tokens, here_x * short, short)
        blocks = []
        for step in range(1, n_ctx):
            sent = shift_ctx(sent, 1, n_ctx)
            if step == 1:
                sent = tie(sent, *columns[1:])
            elif step == 2:
                sent = tie(sent, weight, blocks[0], out_all)
            blocks.append(in_order(here_x, sent, swap(sent, "tp")).reshape(rows, width))
        blocks.append(tokens)
        raws = [product(block, weight) for block in blocks]
        raw = jnp.concatenate(raws)
        sums = [
            jnp.stack(
                [jnp.sum(jnp.square(r[:, c * wide : (c + 1) * wide]), axis=-1) for c in range(2)]
            )
            for r in raws
        ]
        squares = by_source([sums[-1]] + sums[:-1], ctx).swapaxes(0, 1).reshape(2, n_ctx * rows)
        size = math.gcd(rows, 384)
        order = jnp.arange(n_ctx * rows // size, dtype=jnp.int32)
        block_of, inside = order // (rows // size), order % (rows // size)
        place = lax.rem(ctx - block_of - 1 + n_ctx, n_ctx) * (rows // size) + inside
        place = place.astype(jnp.int32)

        starts = doc_starts(segments[None])
        places = jnp.arange(n_ctx * rows, dtype=jnp.int32) - starts[0]
        first_head = ctx * wide
        first_block = jnp.zeros((1,), jnp.int32)

        def sum_stats(stats):
            return lax.psum(stats, ("ctx", "tp"))

        ready = (sent, blocks[1])
    else:
        heads = att // HD
        wide = att
        weight = gather(query_weight, key_weight, value_weight)
        raw = product(both(inner_tokens), weight)
        ready = ()
        squares = jnp.stack(
            [jnp.sum(jnp.square(raw[:, c * wide : (c + 1) * wide]), axis=-1) for c in range(2)]
        )
        place = jnp.arange(2 * rows // math.gcd(rows, 384), dtype=jnp.int32)
        starts = doc_starts(both(segments[None]))
        here = lax.dynamic_slice_in_dim(starts, ctx * rows, rows, axis=1)
        places = (ctx * rows + jnp.arange(rows, dtype=jnp.int32)[None, :] - here).reshape(-1)
        first_head = core * wide
        first_block = ctx.astype(jnp.int32)[None]

        def sum_stats(stats):
            split = stats.reshape(2, 2, rows)
            ordered = jnp.where(core == 0, split, split[:, ::-1])
            total = lax.psum(ordered, ("core", "tp"))
            return jnp.where(core == 0, total, total[:, ::-1]).reshape(stats.shape)

    gate_line = gather(gate_weight, after=ready, axes="ctx")
    gate_other = swap(gate_line, "y")
    gate_all = in_order(here_y, gate_line, gate_other).reshape(width, -1)
    up_down_all = gather(up_weight, down_weight.T, after=ready)

    my_gains = jnp.stack(
        [
            lax.dynamic_slice_in_dim(query_gain, first_head, wide),
            lax.dynamic_slice_in_dim(key_gain, first_head, wide),
        ]
    )[:, None, :]
    cosine, sine = angles(places)
    edges = starts.reshape(starts.shape[0], n_ctx, rows)
    edges = (edges[:, :, 0], edges[:, :, -1])
    scales = lax.rsqrt(sum_stats(squares) / width + EPSILON)[:, :, None]
    turned = turn(place, raw, scales, my_gains, cosine, sine, heads)
    if by_sequence:
        keys, values = (turned, heads), (turned, 2 * heads)
    else:

        def whole_sequences(columns):
            line = lax.all_gather(columns.reshape(2, rows, wide), "ctx", axis=1, tiled=True)
            return line.reshape(-1, wide)

        keys = (whole_sequences(turned[:, wide : 2 * wide]), 0)
        values = (whole_sequences(turned[:, 2 * wide :]), 0)
    out_att, lse = attend(
        first_block, starts, edges, heads, rows, (turned, 0), keys, values
    )
    if by_sequence:
        received = []
        for step in range(n_ctx):
            start = lax.rem(ctx + step, n_ctx) * rows
            block = lax.dynamic_slice_in_dim(out_att, start, rows)
            received.append(shift_ctx(block, step, n_ctx) if step else block)
        received[-1] = tie(received[-1], gate_other)
        twice = jnp.concatenate(received[::-1] + received[::-1], axis=1)
        own = lax.dynamic_slice_in_dim(twice, (n_ctx - 1 - ctx) * wide, local, axis=1)
        other = swap(lax.dynamic_slice_in_dim(own, (1 - core) * att, att, axis=1), "core")
        attended = jnp.concatenate([lax.dynamic_slice_in_dim(own, core * att, att, axis=1), other])
    else:
        attended = out_att

    spans = [slice(0, short), slice(short, rows)]
    attended = [chunk(attended, j) for j in range(2)]
    parts = [contract_cols(rows_part, out_all).astype(bf16) for rows_part in attended]
    attn_sums = [open_sum(part) for part in parts]

    def forward(j, attn_rows):
        attn_scale = lax.rsqrt(jnp.mean(attn_rows * attn_rows, axis=-1, keepdims=True) + EPSILON)
        attn_unit = attn_rows * attn_scale
        hidden_rows = inner_tokens[spans[j]].astype(f32) + attn_unit * attn_gain
        hidden_low = both(hidden_rows.astype(bf16))
        gate_rows, up_rows, act_low = feed(hidden_low, gate_all, up_down_all)
        part = project(act_low, up_down_all)
        return part, act_low, hidden_low, hidden_rows, attn_scale, attn_unit, gate_rows, up_rows

    def turn_norm(j, state, mlp_rows):
        hidden_rows = state[3]
        mlp_scale = lax.rsqrt(jnp.mean(mlp_rows * mlp_rows, axis=-1, keepdims=True) + EPSILON)
        mlp_unit = mlp_rows * mlp_scale
        output = (hidden_rows + mlp_unit * mlp_gain).astype(bf16)
        grad_out = inner_cotangent[spans[j]].astype(f32)
        gain_part = jnp.sum(grad_out * mlp_unit, axis=0)
        scaled_out = grad_out * mlp_gain
        inner_out = jnp.mean(scaled_out * mlp_unit, axis=-1, keepdims=True)
        grad_mlp_low = both((mlp_scale * (scaled_out - mlp_unit * inner_out)).astype(bf16))
        return grad_mlp_low, output, gain_part

    def turn_back(state, grad_mlp_low):
        gate_rows, up_rows = state[6:]
        grad_gate_low, grad_up_low = feed_back(grad_mlp_low, up_down_all, gate_rows, up_rows)
        back = project_both(grad_gate_low, grad_up_low, gate_all, up_down_all)
        return back, grad_gate_low, grad_up_low

    def close_back(j, state, back_rows):
        attn_scale, attn_unit = state[4], state[5]
        grad_hidden = inner_cotangent[spans[j]].astype(f32) + back_rows
        gain_part = jnp.sum(grad_hidden * attn_unit, axis=0)
        scaled_hidden = grad_hidden * attn_gain
        inner_hidden = jnp.mean(scaled_hidden * attn_unit, axis=-1, keepdims=True)
        grad_attn_low = both((attn_scale * (scaled_hidden - attn_unit * inner_hidden)).astype(bf16))
        grad_att = product(grad_attn_low, out_all).astype(bf16)
        return grad_att, grad_attn_low, grad_hidden, gain_part

    fore_a = forward(0, close_sum(*attn_sums[0]))
    mlp_a = open_sum(fore_a[0])
    fore_b = forward(1, close_sum(attn_sums[1][0], tie(attn_sums[1][1], fore_a[0])))
    mlp_b = open_sum(fore_b[0])
    norm_a = turn_norm(0, fore_a, close_sum(mlp_a[0], tie(mlp_a[1], fore_b[0])))
    back_a = turn_back(fore_a, norm_a[0])
    hid_a = open_sum(back_a[0])
    norm_b = turn_norm(1, fore_b, close_sum(mlp_b[0], tie(mlp_b[1], back_a[0])))
    down_grad = outer((norm_a[0], tie(norm_b[0], hid_a[0])), (fore_a[1], fore_b[1]))
    down_low = scatter(down_grad)
    back_b = turn_back(fore_b, tie(norm_b[0], down_grad))
    hid_b = open_sum(back_b[0])
    hiddens = (fore_a[2], fore_b[2])
    close_a = close_back(0, fore_a, close_sum(hid_a[0], tie(hid_a[1], back_b[0])))
    gate_grad = outer(hiddens, (back_a[1], back_b[1]))
    gate_low = scatter(gate_grad)
    close_b = close_back(1, fore_b, close_sum(hid_b[0], tie(hid_b[1], gate_grad)))
    grad_att = unchunk([close_a[0], close_b[0]])

    def later(values):
        return tie(values, own) if by_sequence else values

    if by_sequence:
        own = beside(core, grad_att[:rows], swap(grad_att[rows:], "core"))
        received = []
        for step in range(n_ctx):
            start = lax.rem(ctx + step, n_ctx) * wide
            block = lax.dynamic_slice_in_dim(own, start, wide, axis=1)
            received.append(shift_ctx(block, step, n_ctx) if step else block)
        grad_att = by_source(received, ctx).reshape(n_ctx * rows, wide)
    up_low = scatter(outer(hiddens, (back_a[2], tie(back_b[2], back_b[0]))))
    out_theirs, out_mine = (
        outer(
            [
                lax.dynamic_slice_in_dim(close[1], index * half, half, axis=1)
                for close in (close_a, close_b)
            ],
            (attended[0], later(attended[1])),
        )
        for index in (1 - here_y, here_y)
    )
    out_total = (out_mine.astype(f32) + swap(out_theirs, "y").astype(f32)).astype(bf16)
    out_sent = []
    for step in range(n_ctx):
        start = lax.rem(ctx + step, n_ctx) * 2 * piece
        block = lax.dynamic_slice_in_dim(out_total, start, 2 * piece)
        out_sent.append(shift_ctx(block, step, n_ctx) if step else block)
    out_low = sum(block.astype(f32) for block in out_sent).astype(bf16)
    dq, dk, dv = attend_back(
        first_block, starts, edges, heads, rows, lse, (turned, 0), out_att, grad_att, keys, values
    )
    if not by_sequence:

        def own_rows(grads):
            split = grads.reshape(2, n_ctx * rows, wide)
            low = lax.psum_scatter(split, "ctx", scatter_dimension=1, tiled=True)
            return low.reshape(2 * rows, wide)

        dk, dv = own_rows(dk), own_rows(dv)
    scaled, inner, gain_sums = unturn(
        place, dq, dk, raw, scales, my_gains, cosine, sine, heads
    )
    inner = sum_stats(inner[:, :, 0])[:, :, None] / width
    grad_qkv = norm_back(place, scaled, raw, scales, inner, dv, heads)

    spread = jnp.zeros((2, local), f32)
    spread = lax.dynamic_update_slice(spread, gain_sums[:, 0], (jnp.int32(0), first_head))
    gains = jnp.concatenate([spread.reshape(-1), close_a[3] + close_b[3], norm_a[2] + norm_b[2]])
    if by_sequence:
        weight_halves = weight.reshape(2, half, 3 * wide)
        weight_mine = lax.dynamic_index_in_dim(weight_halves, here_x, 0, keepdims=False)
        weight_theirs = lax.dynamic_index_in_dim(weight_halves, 1 - here_x, 0, keepdims=False)
        grad_blocks = [grad_qkv[step * rows : (step + 1) * rows] for step in range(n_ctx)]
        others = [
            swap(contract_cols(block, weight_theirs).astype(bf16), "tp") for block in grad_blocks
        ]

        def y_half(index, after):
            tied = tie(grad_qkv, after)
            return sum(
                contract_rows(
                    lax.dynamic_slice_in_dim(block, index * half, half, axis=1),
                    tied[step * rows : (step + 1) * rows],
                )
                for step, block in enumerate(blocks)
            )

        terms = []
        for step in range(n_ctx):
            block = grad_blocks[step]
            if step == n_ctx - 1:
                block = tie(block, qkv_theirs)
            other = tie(others[step], terms[0]) if step == 2 else others[step]
            term = contract_cols(block, weight_mine) + other.astype(f32)
            if step < n_ctx - 1:
                low = term.astype(bf16)
                if step == 1:
                    qkv_theirs = y_half(1 - here_y, low).astype(bf16)
                term = shift_ctx(low, -1 - step, n_ctx)
            terms.append(term)
        qkv_total = y_half(here_y, qkv_theirs) + swap(qkv_theirs, "y").astype(f32)
        split = qkv_total.reshape(2, n_ctx * piece, 3 * wide)
        mine = lax.dynamic_index_in_dim(split, core, 0, keepdims=False)
        qkv_low = lax.dynamic_index_in_dim(split, 1 - core, 0, keepdims=False)
        qkv_low = (mine + swap(qkv_low.astype(bf16), "core").astype(f32)).astype(bf16)
        received = []
        for step in range(n_ctx):
            start = lax.rem(ctx + step, n_ctx) * piece
            block = lax.dynamic_slice_in_dim(qkv_low, start, piece)
            received.append(shift_ctx(block, step, n_ctx) if step else block)
        gains = lax.psum(tie(gains, low), ("y", "core", "ctx"))
        terms[-1] = tie(terms[-1], gains, *received[1:])
        dx = lowered(sum(term.astype(f32) for term in terms))
        dx_rows = beside(here_x, dx, swap(dx, "tp")).astype(f32)
        down_low, gate_low, up_low = (tie(values, dx) for values in (down_low, gate_low, up_low))
        lines = by_source(received, ctx)
        qkv_shards = [
            jnp.concatenate([lines[n, :, c * wide : (c + 1) * wide] for n in range(n_ctx)], axis=1)
            .astype(f32)
            for c in range(3)
        ]
    else:
        gains = lax.psum(gains, ("y", "core", "ctx"))
        grad_rows = [chunk(grad_qkv, j) for j in range(2)]
        token_rows = both(inner_tokens)
        token_rows = [chunk(token_rows, j) for j in range(2)]
        qkv_shards = [
            own_share(scatter(outer(token_rows, [r[:, c * wide : (c + 1) * wide] for r in grad_rows])))
            for c in range(3)
        ]
        sums = [open_sum(contract_cols(rows_part, weight).astype(bf16)) for rows_part in grad_rows]
        dx_rows = reorder(jnp.concatenate([close_sum(*parts) for parts in sums]), outward)
    grad_tokens = reorder(later(jnp.concatenate([close_a[2], close_b[2]])), outward) + dx_rows

    cuts = [local, 2 * local, 2 * local + width]
    query_gain_grad, key_gain_grad, attn_gain_grad, mlp_gain_grad = jnp.split(gains, cuts)
    attn_gain_grad, mlp_gain_grad = (
        jnp.concatenate([gain[n * piece : (n + 1) * piece] for n in outward])
        for gain in (attn_gain_grad, mlp_gain_grad)
    )
    return (
        reorder(later(jnp.concatenate([norm_a[1], norm_b[1]])), outward),
        grad_tokens,
        *qkv_shards,
        own_share(out_low).T,
        own_share(gate_low),
        own_share(up_low),
        own_share(down_low).T,
        query_gain_grad,
        key_gain_grad,
        attn_gain_grad,
        mlp_gain_grad,
    )


def solution(mesh):
    sizes = {"y": mesh.shape["dp"] // 2, "core": 2, "ctx": mesh.shape["ctx"], "tp": mesh.shape["tp"]}
    split = Mesh(mesh.devices.reshape(tuple(sizes.values())), tuple(sizes))
    dp = ("y", "core")
    every = ("y", "core", "ctx")
    in_specs = (
        P(every, None),
        P(dp),
        P(every, "tp"),
        P(every, "tp"),
        P(every, "tp"),
        P("tp", every),
        P(every, "tp"),
        P(every, "tp"),
        P("tp", every),
        P("tp"),
        P("tp"),
        P(),
        P(),
        P(every, None),
    )
    out_specs = (
        P(every, None),
        P(every, None),
        P(every, "tp"),
        P(every, "tp"),
        P(every, "tp"),
        P("tp", every),
        P(every, "tp"),
        P(every, "tp"),
        P("tp", every),
        P("tp"),
        P("tp"),
        P(),
        P(),
    )
    return jax.shard_map(
        functools.partial(body, sizes=sizes),
        mesh=split,
        in_specs=in_specs,
        out_specs=out_specs,
        check_vma=False,
    )
```

```python
import functools
import math

import jax
import jax.numpy as jnp
from jax import lax
from jax.experimental import pallas as pl
from jax.experimental.pallas import tpu as pltpu
from jax.sharding import Mesh
from jax.sharding import PartitionSpec as P

HD = 128
EPSILON = 1e-06
ROPE_BASE = 500000.0
MASKED = -1e30
SCALING = HD**-0.5
LOG2E = math.log2(math.e)
BLOCK_K = 256
VMEM_LIMIT = 48 << 20
bf16 = jnp.bfloat16
f32 = jnp.float32


def cost(products, moved):
    return pl.CostEstimate(flops=products, bytes_accessed=moved // 2, transcendentals=0)


def dims(left, right, over):
    return lax.dot_general(left, right, (over, ((), ())), preferred_element_type=f32)


def product(left, right):
    return dims(left, right, ((1,), (0,)))


def contract_rows(left, right):
    return dims(left, right, ((0,), (0,)))


def contract_cols(left, right):
    return dims(left, right, ((1,), (1,)))


def key_steps(block, low, high, bk, per_block):
    end = block * per_block
    begin = jnp.minimum(low // bk, end)
    clear = jnp.minimum((high + bk - 1) // bk, end)
    return begin, clear, end


def diagonal(step, scores, start, first, bk):
    key = step * bk + lax.broadcasted_iota(jnp.int32, scores.shape, 0)
    place = step * bk + lax.broadcasted_iota(jnp.int32, scores.shape, 1)
    return jnp.where((key <= place) & (key + first >= start), scores, MASKED)


def attend_kernel(
    first_ref, low_ref, high_ref, start_ref, q_ref, k_ref, v_ref, o_ref, lse_ref, *, bk
):
    size = q_ref.shape[0]
    per_block = size // bk
    block = first_ref[0] + pl.program_id(2)
    sequence = pl.program_id(1)
    queries = q_ref[...]
    start = start_ref[0]

    def update(carry, scores, values):
        peak, total, acc = carry
        new_peak = jnp.maximum(peak, jnp.max(scores, axis=0, keepdims=True))
        weights = jnp.exp2(scores - new_peak)
        shrink = jnp.exp2(peak - new_peak)
        total = total * shrink + jnp.sum(weights, axis=0, keepdims=True)
        acc = acc * shrink + contract_rows(values, weights.astype(bf16))
        return new_peak, total, acc

    def clear_step(j, carry):
        rows = pl.ds(pl.multiple_of(j * bk, bk), bk)
        return update(carry, contract_cols(k_ref[rows, :], queries), v_ref[rows, :])

    def masked_step(j, carry):
        rows = pl.ds(pl.multiple_of(j * bk, bk), bk)
        scores = contract_cols(k_ref[rows, :], queries)
        key = j * bk + lax.broadcasted_iota(jnp.int32, (bk, 1), 0)
        return update(carry, jnp.where(key >= start, scores, MASKED), v_ref[rows, :])

    begin, clear, end = key_steps(
        block, low_ref[sequence, block], high_ref[sequence, block], bk, per_block
    )
    carry = (
        jnp.full((1, size), MASKED, f32),
        jnp.zeros((1, size), f32),
        jnp.zeros((HD, size), f32),
    )
    carry = lax.fori_loop(begin, clear, masked_step, carry)
    carry = lax.fori_loop(jnp.maximum(begin, clear), end, clear_step, carry)
    for step in range(per_block):
        cut = step * bk
        rows = pl.ds(pl.multiple_of(block * size + cut, bk), bk)
        scores = contract_cols(k_ref[rows, :], queries[cut:])
        scores = diagonal(step, scores, start[:, cut:], block * size, bk)
        right = update(tuple(part[:, cut:] for part in carry), scores, v_ref[rows, :])
        if cut:
            right = tuple(
                jnp.concatenate([part[:, :cut], new], axis=1) for part, new in zip(carry, right)
            )
        carry = right
    peak, total, acc = carry
    o_ref[...] = (acc / total).T.astype(bf16)
    lse_ref[0] = peak + jnp.log2(total)


def attend(first, starts, edges, heads, size, query, key, value):
    sequences, length = starts.shape
    slots = query[0].shape[0] // (sequences * size)
    rows = query[0].shape[0]

    def part(offset):
        return pl.BlockSpec((size, HD), lambda g, b, s, *refs: (b * slots + s, offset + g))

    def whole(offset):
        return pl.BlockSpec((length, HD), lambda g, b, s, *refs: (b, offset + g))

    return pl.pallas_call(
        functools.partial(attend_kernel, bk=min(BLOCK_K, size)),
        grid_spec=pltpu.PrefetchScalarGridSpec(
            num_scalar_prefetch=3,
            grid=(heads, sequences, slots),
            in_specs=[
                pl.BlockSpec((1, 1, size), lambda g, b, s, first, *refs: (b, 0, first[0] + s)),
                part(query[1]),
                whole(key[1]),
                whole(value[1]),
            ],
            out_specs=[
                part(0),
                pl.BlockSpec((1, 1, size), lambda g, b, s, *refs: (g, 0, b * slots + s)),
            ],
        ),
        out_shape=[
            jax.ShapeDtypeStruct((rows, heads * HD), bf16),
            jax.ShapeDtypeStruct((heads, 1, rows), f32),
        ],
        cost_estimate=cost(4 * HD * heads * rows * length, 0),
        compiler_params=pltpu.CompilerParams(vmem_limit_bytes=VMEM_LIMIT),
        name="attend",
    )(first, *edges, starts[:, None, :], query[0], key[0], value[0])


def attend_back_kernel(
    first_ref,
    low_ref,
    high_ref,
    start_ref,
    lse_ref,
    q_ref,
    o_ref,
    do_ref,
    k_ref,
    v_ref,
    dq_ref,
    dk_ref,
    dv_ref,
    dk_sum,
    dv_sum,
    *,
    bk,
):
    size = q_ref.shape[0]
    per_block = size // bk
    block = first_ref[0] + pl.program_id(2)
    sequence = pl.program_id(1)
    queries = q_ref[...]
    grads = do_ref[...]
    start = start_ref[0]
    lse = lse_ref[0]
    delta = jnp.sum((grads.astype(f32) * o_ref[...].astype(f32)).T, axis=0, keepdims=True)

    @pl.when(pl.program_id(2) == 0)
    def _():
        dk_sum[...] = jnp.zeros_like(dk_sum)
        dv_sum[...] = jnp.zeros_like(dv_sum)

    def update(dq, scores, rows, cut):
        probs = jnp.exp2(scores - lse[:, cut:])
        dv_sum[rows, :] += product(probs.astype(bf16), grads[cut:])
        dprobs = contract_cols(v_ref[rows, :], grads[cut:])
        dscores = (probs * (dprobs - delta[:, cut:])).astype(bf16)
        dk_sum[rows, :] += product(dscores, queries[cut:])
        return dq + contract_rows(k_ref[rows, :], dscores)

    def clear_step(j, dq):
        rows = pl.ds(pl.multiple_of(j * bk, bk), bk)
        return update(dq, contract_cols(k_ref[rows, :], queries), rows, 0)

    def masked_step(j, dq):
        rows = pl.ds(pl.multiple_of(j * bk, bk), bk)
        scores = contract_cols(k_ref[rows, :], queries)
        key = j * bk + lax.broadcasted_iota(jnp.int32, (bk, 1), 0)
        return update(dq, jnp.where(key >= start, scores, MASKED), rows, 0)

    begin, clear, end = key_steps(
        block, low_ref[sequence, block], high_ref[sequence, block], bk, per_block
    )
    dq = jnp.zeros((HD, size), f32)
    dq = lax.fori_loop(begin, clear, masked_step, dq)
    dq = lax.fori_loop(jnp.maximum(begin, clear), end, clear_step, dq)
    for step in range(per_block):
        cut = step * bk
        rows = pl.ds(pl.multiple_of(block * size + cut, bk), bk)
        scores = contract_cols(k_ref[rows, :], queries[cut:])
        scores = diagonal(step, scores, start[:, cut:], block * size, bk)
        right = update(dq[:, cut:], scores, rows, cut)
        dq = jnp.concatenate([dq[:, :cut], right], axis=1) if cut else right
    dq_ref[...] = (dq.T * SCALING).astype(bf16)

    @pl.when(pl.program_id(2) == pl.num_programs(2) - 1)
    def _():
        dk_ref[...] = (dk_sum[...] * (1.0 / LOG2E)).astype(bf16)
        dv_ref[...] = dv_sum[...].astype(bf16)


def attend_back(first, starts, edges, heads, size, lse, query, out, grad, key, value):
    sequences, length = starts.shape
    rows = query[0].shape[0]
    slots = rows // (sequences * size)

    def part(offset):
        return pl.BlockSpec((size, HD), lambda g, b, s, *refs: (b * slots + s, offset + g))

    def whole(offset):
        return pl.BlockSpec((length, HD), lambda g, b, s, *refs: (b, offset + g))

    return pl.pallas_call(
        functools.partial(attend_back_kernel, bk=min(BLOCK_K, size)),
        grid_spec=pltpu.PrefetchScalarGridSpec(
            num_scalar_prefetch=3,
            grid=(heads, sequences, slots),
            in_specs=[
                pl.BlockSpec((1, 1, size), lambda g, b, s, first, *refs: (b, 0, first[0] + s)),
                pl.BlockSpec((1, 1, size), lambda g, b, s, *refs: (g, 0, b * slots + s)),
                part(query[1]),
                part(0),
                part(0),
                whole(key[1]),
                whole(value[1]),
            ],
            out_specs=[part(0), whole(0), whole(0)],
            scratch_shapes=[pltpu.VMEM((length, HD), f32)] * 2,
        ),
        out_shape=[
            jax.ShapeDtypeStruct((rows, heads * HD), bf16),
            jax.ShapeDtypeStruct((sequences * length, heads * HD), bf16),
            jax.ShapeDtypeStruct((sequences * length, heads * HD), bf16),
        ],
        cost_estimate=cost(5 * HD * heads * rows * length, 0),
        compiler_params=pltpu.CompilerParams(vmem_limit_bytes=VMEM_LIMIT),
        name="attend_back",
    )(first, *edges, starts[:, None, :], lse, query[0], out, grad, key[0], value[0])


def turn_kernel(place_ref, raw_ref, scale_ref, gain_ref, cos_ref, sin_ref, out_ref, *, heads):
    for c in range(3):
        for h in range(heads):
            cols = slice((c * heads + h) * HD, (c * heads + h + 1) * HD)
            values = raw_ref[:, cols]
            if c < 2:
                values = values * scale_ref[c] * gain_ref[c, :, h * HD : (h + 1) * HD]
                values = values * cos_ref[...] + pltpu.roll(values, HD // 2, 1) * sin_ref[...]
            if c == 0:
                values = values * (SCALING * LOG2E)
            out_ref[:, cols] = values.astype(bf16)


def turn(place, raw, scales, gains, cosine, sine, heads):
    rows = raw.shape[0]
    size = rows // place.shape[0]
    return pl.pallas_call(
        functools.partial(turn_kernel, heads=heads),
        grid_spec=pltpu.PrefetchScalarGridSpec(
            num_scalar_prefetch=1,
            grid=(rows // size,),
            in_specs=[
                pl.BlockSpec((size, 3 * heads * HD), lambda i, place: (place[i], 0)),
                pl.BlockSpec((2, size, 1), lambda i, place: (0, i, 0)),
                pl.BlockSpec((2, 1, heads * HD), lambda i, place: (0, 0, 0)),
                pl.BlockSpec((size, HD), lambda i, place: (i, 0)),
                pl.BlockSpec((size, HD), lambda i, place: (i, 0)),
            ],
            out_specs=pl.BlockSpec((size, 3 * heads * HD), lambda i, place: (i, 0)),
        ),
        out_shape=jax.ShapeDtypeStruct(raw.shape, bf16),
        cost_estimate=cost(0, 20 * rows * heads * HD),
        compiler_params=pltpu.CompilerParams(vmem_limit_bytes=VMEM_LIMIT),
        name="turn",
    )(place, raw, scales, gains, cosine, sine)


def unturn_kernel(
    place_ref,
    dq_ref,
    dk_ref,
    raw_ref,
    scale_ref,
    gain_ref,
    cos_ref,
    sin_ref,
    out_ref,
    inner_ref,
    sum_ref,
    *,
    heads,
):
    @pl.when(pl.program_id(0) == 0)
    def _():
        sum_ref[...] = jnp.zeros_like(sum_ref)

    for c, grad_ref in enumerate((dq_ref, dk_ref)):
        inner = 0.0
        for h in range(heads):
            head = slice(h * HD, (h + 1) * HD)
            cols = slice((c * heads + h) * HD, (c * heads + h + 1) * HD)
            grad = grad_ref[:, head].astype(f32)
            normed = grad * cos_ref[...] - pltpu.roll(grad, HD // 2, 1) * sin_ref[...]
            unit = raw_ref[:, cols] * scale_ref[c]
            scaled = normed * gain_ref[c, :, head]
            out_ref[:, cols] = scaled
            inner = inner + jnp.sum(scaled * unit, axis=1, keepdims=True)
            sum_ref[c, :, head] += jnp.sum(normed * unit, axis=0, keepdims=True)
        inner_ref[c] = inner


def unturn(place, dq, dk, raw, scales, gains, cosine, sine, heads):
    rows = raw.shape[0]
    size = rows // place.shape[0]
    width = heads * HD
    return pl.pallas_call(
        functools.partial(unturn_kernel, heads=heads),
        grid_spec=pltpu.PrefetchScalarGridSpec(
            num_scalar_prefetch=1,
            grid=(rows // size,),
            in_specs=[
                pl.BlockSpec((size, width), lambda i, place: (i, 0)),
                pl.BlockSpec((size, width), lambda i, place: (i, 0)),
                pl.BlockSpec((size, 3 * width), lambda i, place: (place[i], 0)),
                pl.BlockSpec((2, size, 1), lambda i, place: (0, i, 0)),
                pl.BlockSpec((2, 1, width), lambda i, place: (0, 0, 0)),
                pl.BlockSpec((size, HD), lambda i, place: (i, 0)),
                pl.BlockSpec((size, HD), lambda i, place: (i, 0)),
            ],
            out_specs=[
                pl.BlockSpec((size, 2 * width), lambda i, place: (i, 0)),
                pl.BlockSpec((2, size, 1), lambda i, place: (0, i, 0)),
                pl.BlockSpec((2, 1, width), lambda i, place: (0, 0, 0)),
            ],
        ),
        out_shape=[
            jax.ShapeDtypeStruct((rows, 2 * width), f32),
            jax.ShapeDtypeStruct((2, rows, 1), f32),
            jax.ShapeDtypeStruct((2, 1, width), f32),
        ],
        cost_estimate=cost(0, 32 * rows * width),
        compiler_params=pltpu.CompilerParams(vmem_limit_bytes=VMEM_LIMIT),
        name="unturn",
    )(place, dq, dk, raw, scales, gains, cosine, sine)


def norm_back_kernel(
    place_ref, scaled_ref, raw_ref, scale_ref, inner_ref, dv_ref, out_ref, *, heads
):
    width = heads * HD
    for c in range(2):
        cols = slice(c * width, (c + 1) * width)
        unit = raw_ref[:, cols] * scale_ref[c]
        out_ref[:, cols] = (scale_ref[c] * (scaled_ref[:, cols] - unit * inner_ref[c])).astype(bf16)
    out_ref[:, 2 * width :] = dv_ref[...]


def norm_back(place, scaled, raw, scales, inner, dv, heads):
    rows = raw.shape[0]
    size = rows // place.shape[0]
    width = heads * HD
    return pl.pallas_call(
        functools.partial(norm_back_kernel, heads=heads),
        grid_spec=pltpu.PrefetchScalarGridSpec(
            num_scalar_prefetch=1,
            grid=(rows // size,),
            in_specs=[
                pl.BlockSpec((size, 2 * width), lambda i, place: (i, 0)),
                pl.BlockSpec((size, 3 * width), lambda i, place: (place[i], 0)),
                pl.BlockSpec((2, size, 1), lambda i, place: (0, i, 0)),
                pl.BlockSpec((2, size, 1), lambda i, place: (0, i, 0)),
                pl.BlockSpec((size, width), lambda i, place: (i, 0)),
            ],
            out_specs=pl.BlockSpec((size, 3 * width), lambda i, place: (place[i], 0)),
        ),
        out_shape=jax.ShapeDtypeStruct((rows, 3 * width), bf16),
        cost_estimate=cost(0, 24 * rows * width),
        compiler_params=pltpu.CompilerParams(vmem_limit_bytes=VMEM_LIMIT),
        name="norm_back",
    )(place, scaled, raw, scales, inner, dv)


def reorder_kernel(in_ref, out_ref, *, order):
    size = in_ref.shape[1] // len(order)
    for n, m in enumerate(order):
        out_ref[:, n * size : (n + 1) * size] = in_ref[:, m * size : (m + 1) * size]


def reorder(values, order):
    rows, width = values.shape
    size = math.gcd(rows, 192)
    spec = pl.BlockSpec((size, width), lambda i: (i, 0))
    return pl.pallas_call(
        functools.partial(reorder_kernel, order=order),
        grid=(rows // size,),
        in_specs=[spec],
        out_specs=spec,
        out_shape=jax.ShapeDtypeStruct(values.shape, values.dtype),
        cost_estimate=cost(0, 2 * values.size * values.dtype.itemsize),
        compiler_params=pltpu.CompilerParams(vmem_limit_bytes=VMEM_LIMIT),
        name="reorder",
    )(values)


def outer_kernel(part_ref, left_a, left_b, right_a, right_b, *refs):
    total = contract_rows(left_a[...], right_a[...]) + contract_rows(left_b[...], right_b[...])
    if len(refs) == 2:
        total = total + refs[0][...].astype(f32)
    refs[-1][...] = total.astype(bf16)


def outer(lefts, rights, part, parts=2, add=None):
    rows, high = lefts[0].shape
    high = high // parts
    wide = rights[0].shape[1]
    tall, broad = math.gcd(high, 512), math.gcd(wide, 1024)
    count = high // tall
    left = pl.BlockSpec((rows, tall), lambda i, j, part: (0, part[0] * count + i))
    right = pl.BlockSpec((rows, broad), lambda i, j, part: (0, j))
    out = pl.BlockSpec((tall, broad), lambda i, j, part: (i, j))
    more = () if add is None else (add,)
    return pl.pallas_call(
        outer_kernel,
        grid_spec=pltpu.PrefetchScalarGridSpec(
            num_scalar_prefetch=1,
            grid=(count, wide // broad),
            in_specs=[left, left, right, right] + [out] * len(more),
            out_specs=out,
        ),
        out_shape=jax.ShapeDtypeStruct((high, wide), bf16),
        cost_estimate=cost(2 * rows * high * wide, 0),
        compiler_params=pltpu.CompilerParams(vmem_limit_bytes=VMEM_LIMIT),
        name="outer",
    )(part.astype(jnp.int32)[None], *lefts, *rights, *more)


def feed_kernel(hidden_ref, gate_ref, up_ref, gate_out, up_out, act_out):
    gate = product(hidden_ref[...], gate_ref[...])
    up = product(hidden_ref[...], up_ref[...])
    gate_out[...] = gate.astype(bf16)
    up_out[...] = up.astype(bf16)
    act_out[...] = (gate * jax.nn.sigmoid(gate) * up).astype(bf16)


def feed(hidden, gate, up_down):
    rows, width = hidden.shape
    units = gate.shape[1]
    wide = math.gcd(units, 512)
    out = pl.BlockSpec((rows, wide), lambda j: (0, j))
    return pl.pallas_call(
        feed_kernel,
        grid=(units // wide,),
        in_specs=[
            pl.BlockSpec((rows, width), lambda j: (0, 0)),
            pl.BlockSpec((width, wide), lambda j: (0, j)),
            pl.BlockSpec((width, wide), lambda j: (0, j)),
        ],
        out_specs=[out, out, out],
        out_shape=[jax.ShapeDtypeStruct((rows, units), bf16)] * 3,
        cost_estimate=cost(2 * rows * width * units, 0),
        compiler_params=pltpu.CompilerParams(vmem_limit_bytes=VMEM_LIMIT),
        name="feed",
    )(hidden, gate, up_down)


def project_kernel(left_ref, right_ref, out_ref):
    out_ref[...] = contract_cols(left_ref[...], right_ref[...]).astype(bf16)


def project(act, up_down):
    rows, units = act.shape
    width = up_down.shape[0]
    wide = math.gcd(width, 512)
    return pl.pallas_call(
        project_kernel,
        grid=(width // wide,),
        in_specs=[
            pl.BlockSpec((rows, units), lambda j: (0, 0)),
            pl.BlockSpec((wide, units), lambda j: (j, 1)),
        ],
        out_specs=pl.BlockSpec((rows, wide), lambda j: (0, j)),
        out_shape=jax.ShapeDtypeStruct((rows, width), bf16),
        cost_estimate=cost(rows * units * width, 0),
        compiler_params=pltpu.CompilerParams(vmem_limit_bytes=VMEM_LIMIT),
        name="project",
    )(act, up_down)


def feed_back_kernel(grad_ref, down_ref, gate_ref, up_ref, gate_out, up_out):
    grad = product(grad_ref[...], down_ref[...])
    gate = gate_ref[...].astype(f32)
    sigmoid = jax.nn.sigmoid(gate)
    gate_out[...] = (
        grad * up_ref[...].astype(f32) * (sigmoid * (1.0 + gate * (1.0 - sigmoid)))
    ).astype(bf16)
    up_out[...] = (grad * (gate * sigmoid)).astype(bf16)


def feed_back(grad, up_down, gate, up):
    rows, width = grad.shape
    units = gate.shape[1]
    wide = math.gcd(units, 512)
    count = units // wide
    part = pl.BlockSpec((rows, wide), lambda j: (0, j))
    return pl.pallas_call(
        feed_back_kernel,
        grid=(count,),
        in_specs=[
            pl.BlockSpec((rows, width), lambda j: (0, 0)),
            pl.BlockSpec((width, wide), lambda j: (0, count + j)),
            part,
            part,
        ],
        out_specs=[part, part],
        out_shape=[jax.ShapeDtypeStruct((rows, units), bf16)] * 2,
        cost_estimate=cost(rows * width * units, 0),
        compiler_params=pltpu.CompilerParams(vmem_limit_bytes=VMEM_LIMIT),
        name="feed_back",
    )(grad, up_down, gate, up)


def project_both_kernel(gate_grad, up_grad, gate_ref, up_ref, out_ref):
    total = contract_cols(gate_grad[...], gate_ref[...]) + contract_cols(up_grad[...], up_ref[...])
    out_ref[...] = total.astype(bf16)


def project_both(gate_grad, up_grad, gate, up_down):
    rows, units = gate_grad.shape
    width = gate.shape[0]
    wide = math.gcd(width, 512)
    left = pl.BlockSpec((rows, units), lambda j: (0, 0))
    return pl.pallas_call(
        project_both_kernel,
        grid=(width // wide,),
        in_specs=[
            left,
            left,
            pl.BlockSpec((wide, units), lambda j: (j, 0)),
            pl.BlockSpec((wide, units), lambda j: (j, 0)),
        ],
        out_specs=pl.BlockSpec((rows, wide), lambda j: (0, j)),
        out_shape=jax.ShapeDtypeStruct((rows, width), bf16),
        cost_estimate=cost(2 * rows * units * width, 0),
        compiler_params=pltpu.CompilerParams(vmem_limit_bytes=VMEM_LIMIT),
        name="project_both",
    )(gate_grad, up_grad, gate, up_down)


def tie_kernel(*refs):
    pass


def tie(values, *others):
    return pl.pallas_call(
        tie_kernel,
        in_specs=[pl.BlockSpec(memory_space=pl.ANY)] * (1 + len(others)),
        out_specs=pl.BlockSpec(memory_space=pl.ANY),
        out_shape=jax.ShapeDtypeStruct(values.shape, values.dtype),
        input_output_aliases={0: 0},
        cost_estimate=cost(0, 0),
        name="tie",
    )(values, *others)


def doc_starts(doc_ids):
    row_index = jnp.arange(doc_ids.shape[-1], dtype=jnp.int32)
    is_start = jnp.concatenate(
        [jnp.ones_like(doc_ids[:, :1], dtype=bool), doc_ids[:, 1:] != doc_ids[:, :-1]], axis=1
    )
    return lax.cummax(jnp.where(is_start, row_index[None, :], 0), axis=1)


def angles(places):
    frequency = ROPE_BASE ** (-(jnp.arange(HD // 2, dtype=f32) * 2.0 / HD))
    phases = places.astype(f32)[:, None] * frequency[None, :]
    cosine, sine = jnp.cos(phases), jnp.sin(phases)
    return (
        jnp.concatenate([cosine, cosine], axis=-1),
        jnp.concatenate([-sine, sine], axis=-1),
    )


def swap(values, axis):
    return lax.ppermute(values, axis, [(0, 1), (1, 0)])


def shift_ctx(values, steps, size):
    return lax.ppermute(values, "ctx", [(i, (i + steps) % size) for i in range(size)])


def by_source(received, me):
    size = len(received)
    turned = jnp.stack(received[::-1] + received[::-1])
    return lax.dynamic_slice_in_dim(turned, size - 1 - me, size, axis=0)


def in_order(index, mine, theirs):
    return jnp.where(index == 0, jnp.stack([mine, theirs]), jnp.stack([theirs, mine]))


def beside(index, mine, theirs):
    first = jnp.where(index == 0, mine, theirs)
    second = jnp.where(index == 0, theirs, mine)
    return jnp.concatenate([first, second], axis=1)


def lowered(values):
    return lax.reduce_precision(values, 8, 7).astype(bf16)


def body(
    tokens,
    segments,
    query_weight,
    key_weight,
    value_weight,
    out_weight,
    gate_weight,
    up_weight,
    down_weight,
    query_gain,
    key_gain,
    attn_gain,
    mlp_gain,
    cotangent,
    *,
    sizes,
):
    core = lax.axis_index("core")
    ctx = lax.axis_index("ctx")
    here_y = lax.axis_index("y")
    here_x = lax.axis_index("tp")
    n_ctx, n_tp = sizes["ctx"], sizes["tp"]
    rows, width = tokens.shape
    piece = query_weight.shape[0]
    local = query_weight.shape[1]
    att = local // 2
    half = width // 2
    short = rows // 2

    def column_half(values, index):
        size = values.shape[1] // 2
        return lax.dynamic_slice_in_dim(values, index * size, size, axis=1)

    def number(y, c, z):
        return (y * 2 + c) * n_ctx + z

    inward = [number(y, c, z) for y in range(2) for z in range(n_ctx) for c in range(2)]
    outward = [inward.index(n) for n in range(4 * n_ctx)]

    def gather(*shards, after=(), axes=("y", "ctx")):
        mine = jnp.concatenate([column_half(shard, core) for shard in shards], axis=1)
        theirs = jnp.concatenate([column_half(shard, 1 - core) for shard in shards], axis=1)
        pair = in_order(core, mine, swap(theirs, "core")).reshape(2 * piece, -1)
        if after:
            pair = tie(pair, *after)
        return lax.all_gather(pair, axes, axis=0, tiled=True)

    def scatter(grad, axes="ctx"):
        return lax.psum_scatter(grad, axes, scatter_dimension=0, tiled=True)

    def own_share(low):
        mine = lax.dynamic_slice_in_dim(low, core * piece, piece)
        theirs = swap(lax.dynamic_slice_in_dim(low, (1 - core) * piece, piece), "core")
        return beside(core, mine, theirs).astype(f32)

    def both(values):
        return jnp.concatenate([values, swap(values, "core")], axis=0)

    def open_sum(part):
        part = part.reshape(2, -1, width)
        total = part[0].astype(f32) + swap(part[1], "core").astype(f32)
        if n_tp == 2:
            low = lowered(total)
            return low, swap(low, "tp")
        low = lax.psum(total.astype(bf16), "tp")
        return low, jnp.zeros_like(low)

    def close_sum(low, other):
        return low.astype(f32) + other.astype(f32)

    def chunk(values, j):
        split = values.reshape(2, rows, -1)[:, j * short : (j + 1) * short]
        return split.reshape(2 * short, -1)

    def unchunk(parts):
        split = [part.reshape(2, short, -1) for part in parts]
        return jnp.concatenate(split, axis=1).reshape(2 * rows, -1)

    by_sequence = n_tp == 2 and (local // HD) % n_ctx == 0
    out_all = gather(out_weight.T)
    inner_tokens = reorder(tokens, inward)
    inner_cotangent = reorder(cotangent, inward)
    attn_gain, mlp_gain = (
        jnp.concatenate([gain[n * piece : (n + 1) * piece] for n in inward])
        for gain in (attn_gain, mlp_gain)
    )

    if by_sequence:
        heads = local // HD // n_ctx
        wide = heads * HD

        def shard_columns(index):
            return jnp.concatenate(
                [
                    lax.dynamic_slice_in_dim(shard, index * wide, wide, axis=1)
                    for shard in (query_weight, key_weight, value_weight)
                ],
                axis=1,
            )

        columns = [shard_columns(ctx)]
        for step in range(1, n_ctx):
            columns.append(shift_ctx(shard_columns(lax.rem(ctx + step, n_ctx)), step, n_ctx))
        weight = by_source(columns, ctx).reshape(n_ctx * piece, 3 * wide)
        weight = in_order(core, weight, swap(weight, "core")).reshape(half, 3 * wide)
        weight = in_order(here_y, weight, swap(weight, "y")).reshape(width, 3 * wide)

        sent = lax.dynamic_slice_in_dim(tokens, here_x * short, short)
        blocks = []
        for step in range(1, n_ctx):
            sent = shift_ctx(sent, 1, n_ctx)
            if step == 1:
                sent = tie(sent, *columns[1:])
            elif step == 2:
                sent = tie(sent, weight, blocks[0], out_all)
            blocks.append(in_order(here_x, sent, swap(sent, "tp")).reshape(rows, width))
        blocks.append(tokens)
        raws = [product(block, weight) for block in blocks]
        raw = jnp.concatenate(raws)
        sums = [
            jnp.stack(
                [jnp.sum(jnp.square(r[:, c * wide : (c + 1) * wide]), axis=-1) for c in range(2)]
            )
            for r in raws
        ]
        squares = by_source([sums[-1]] + sums[:-1], ctx).swapaxes(0, 1).reshape(2, n_ctx * rows)
        size = math.gcd(rows, 384)
        order = jnp.arange(n_ctx * rows // size, dtype=jnp.int32)
        block_of, inside = order // (rows // size), order % (rows // size)
        place = lax.rem(ctx - block_of - 1 + n_ctx, n_ctx) * (rows // size) + inside
        place = place.astype(jnp.int32)

        starts = doc_starts(segments[None])
        places = jnp.arange(n_ctx * rows, dtype=jnp.int32) - starts[0]
        first_head = ctx * wide
        first_block = jnp.zeros((1,), jnp.int32)

        def sum_stats(stats):
            return lax.psum(stats, ("ctx", "tp"))

        ready = (sent, blocks[1])
    else:
        heads = att // HD
        wide = att
        weight = gather(query_weight, key_weight, value_weight)
        raw = product(both(inner_tokens), weight)
        ready = ()
        squares = jnp.stack(
            [jnp.sum(jnp.square(raw[:, c * wide : (c + 1) * wide]), axis=-1) for c in range(2)]
        )
        place = jnp.arange(2 * rows // math.gcd(rows, 384), dtype=jnp.int32)
        starts = doc_starts(both(segments[None]))
        here = lax.dynamic_slice_in_dim(starts, ctx * rows, rows, axis=1)
        places = (ctx * rows + jnp.arange(rows, dtype=jnp.int32)[None, :] - here).reshape(-1)
        first_head = core * wide
        first_block = ctx.astype(jnp.int32)[None]

        def sum_stats(stats):
            split = stats.reshape(2, 2, rows)
            ordered = jnp.where(core == 0, split, split[:, ::-1])
            total = lax.psum(ordered, ("core", "tp"))
            return jnp.where(core == 0, total, total[:, ::-1]).reshape(stats.shape)

    gate_line = gather(gate_weight, after=ready, axes="ctx")
    gate_other = swap(gate_line, "y")
    gate_all = in_order(here_y, gate_line, gate_other).reshape(width, -1)
    up_down_all = gather(up_weight, down_weight.T, after=ready)

    my_gains = jnp.stack(
        [
            lax.dynamic_slice_in_dim(query_gain, first_head, wide),
            lax.dynamic_slice_in_dim(key_gain, first_head, wide),
        ]
    )[:, None, :]
    cosine, sine = angles(places)
    edges = starts.reshape(starts.shape[0], n_ctx, rows)
    edges = (edges[:, :, 0], edges[:, :, -1])
    scales = lax.rsqrt(sum_stats(squares) / width + EPSILON)[:, :, None]
    turned = turn(place, raw, scales, my_gains, cosine, sine, heads)
    if by_sequence:
        keys, values = (turned, heads), (turned, 2 * heads)
    else:

        def whole_sequences(columns):
            line = lax.all_gather(columns.reshape(2, rows, wide), "ctx", axis=1, tiled=True)
            return line.reshape(-1, wide)

        keys = (whole_sequences(turned[:, wide : 2 * wide]), 0)
        values = (whole_sequences(turned[:, 2 * wide :]), 0)
    out_att, lse = attend(
        first_block, starts, edges, heads, rows, (turned, 0), keys, values
    )
    if by_sequence:
        received = []
        for step in range(n_ctx):
            start = lax.rem(ctx + step, n_ctx) * rows
            block = lax.dynamic_slice_in_dim(out_att, start, rows)
            received.append(shift_ctx(block, step, n_ctx) if step else block)
        received[-1] = tie(received[-1], gate_other)
        twice = jnp.concatenate(received[::-1] + received[::-1], axis=1)
        own = lax.dynamic_slice_in_dim(twice, (n_ctx - 1 - ctx) * wide, local, axis=1)
        other = swap(lax.dynamic_slice_in_dim(own, (1 - core) * att, att, axis=1), "core")
        attended = jnp.concatenate([lax.dynamic_slice_in_dim(own, core * att, att, axis=1), other])
    else:
        attended = out_att

    spans = [slice(0, short), slice(short, rows)]
    attended = [chunk(attended, j) for j in range(2)]
    parts = [contract_cols(rows_part, out_all).astype(bf16) for rows_part in attended]
    attn_sums = [open_sum(part) for part in parts]

    def forward(j, attn_rows):
        attn_scale = lax.rsqrt(jnp.mean(attn_rows * attn_rows, axis=-1, keepdims=True) + EPSILON)
        attn_unit = attn_rows * attn_scale
        hidden_rows = inner_tokens[spans[j]].astype(f32) + attn_unit * attn_gain
        hidden_low = both(hidden_rows.astype(bf16))
        gate_rows, up_rows, act_low = feed(hidden_low, gate_all, up_down_all)
        part = project(act_low, up_down_all)
        return part, act_low, hidden_low, hidden_rows, attn_scale, attn_unit, gate_rows, up_rows

    def turn_norm(j, state, mlp_rows):
        hidden_rows = state[3]
        mlp_scale = lax.rsqrt(jnp.mean(mlp_rows * mlp_rows, axis=-1, keepdims=True) + EPSILON)
        mlp_unit = mlp_rows * mlp_scale
        output = (hidden_rows + mlp_unit * mlp_gain).astype(bf16)
        grad_out = inner_cotangent[spans[j]].astype(f32)
        gain_part = jnp.sum(grad_out * mlp_unit, axis=0)
        scaled_out = grad_out * mlp_gain
        inner_out = jnp.mean(scaled_out * mlp_unit, axis=-1, keepdims=True)
        grad_mlp_low = both((mlp_scale * (scaled_out - mlp_unit * inner_out)).astype(bf16))
        return grad_mlp_low, output, gain_part

    def turn_back(state, grad_mlp_low):
        gate_rows, up_rows = state[6:]
        grad_gate_low, grad_up_low = feed_back(grad_mlp_low, up_down_all, gate_rows, up_rows)
        back = project_both(grad_gate_low, grad_up_low, gate_all, up_down_all)
        return back, grad_gate_low, grad_up_low

    def close_back(j, state, back_rows):
        attn_scale, attn_unit = state[4], state[5]
        grad_hidden = inner_cotangent[spans[j]].astype(f32) + back_rows
        gain_part = jnp.sum(grad_hidden * attn_unit, axis=0)
        scaled_hidden = grad_hidden * attn_gain
        inner_hidden = jnp.mean(scaled_hidden * attn_unit, axis=-1, keepdims=True)
        grad_attn_low = both((attn_scale * (scaled_hidden - attn_unit * inner_hidden)).astype(bf16))
        grad_att = product(grad_attn_low, out_all).astype(bf16)
        return grad_att, grad_attn_low, grad_hidden, gain_part

    fore_a = forward(0, close_sum(*attn_sums[0]))
    mlp_a = open_sum(fore_a[0])
    fore_b = forward(1, close_sum(attn_sums[1][0], tie(attn_sums[1][1], fore_a[0])))
    mlp_b = open_sum(fore_b[0])
    norm_a = turn_norm(0, fore_a, close_sum(mlp_a[0], tie(mlp_a[1], fore_b[0])))
    back_a = turn_back(fore_a, norm_a[0])
    hid_a = open_sum(back_a[0])
    norm_b = turn_norm(1, fore_b, close_sum(mlp_b[0], tie(mlp_b[1], back_a[0])))
    down_pairs = ((norm_a[0], tie(norm_b[0], hid_a[0])), (fore_a[1], fore_b[1]))
    down_theirs = outer(*down_pairs, 1 - here_y)
    down_other = swap(down_theirs, "y")
    back_b = turn_back(fore_b, tie(norm_b[0], down_theirs))
    hid_b = open_sum(back_b[0])
    hiddens = (fore_a[2], fore_b[2])
    gate_pairs = (hiddens, (back_a[1], tie(back_b[1], back_b[0])))
    up_pairs = (hiddens, (back_a[2], tie(back_b[2], back_b[0])))
    gate_theirs = outer(*gate_pairs, 1 - here_y)
    close_a = close_back(0, fore_a, close_sum(hid_a[0], tie(hid_a[1], gate_theirs)))
    up_pairs = (hiddens, (back_a[2], tie(back_b[2], close_a[1])))
    up_theirs = outer(*up_pairs, 1 - here_y)
    gate_other, up_other = swap(gate_theirs, "y"), swap(up_theirs, "y")
    down_total = outer(*down_pairs, here_y, add=down_other)
    down_low = scatter(down_total)
    close_b = close_back(1, fore_b, close_sum(hid_b[0], tie(hid_b[1], close_a[0], down_total, up_theirs)))
    grad_att = unchunk([close_a[0], close_b[0]])

    def later(values):
        return tie(values, own) if by_sequence else values

    if by_sequence:
        own = beside(core, grad_att[:rows], swap(grad_att[rows:], "core"))
        received = []
        for step in range(n_ctx):
            start = lax.rem(ctx + step, n_ctx) * wide
            block = lax.dynamic_slice_in_dim(own, start, wide, axis=1)
            received.append(shift_ctx(block, step, n_ctx) if step else block)
        grad_att = by_source(received, ctx).reshape(n_ctx * rows, wide)
    out_pairs = ((close_a[1], close_b[1]), (attended[0], later(attended[1])))
    out_low = scatter(outer(*out_pairs, jnp.int32(0), parts=1), ("y", "ctx"))
    gate_total = outer(hiddens, (back_a[1], later(gate_pairs[1][1])), here_y, add=gate_other)
    gate_low = scatter(gate_total)
    grad_att = tie(grad_att, gate_total)
    dq, dk, dv = attend_back(
        first_block, starts, edges, heads, rows, lse, (turned, 0), out_att, grad_att, keys, values
    )
    if not by_sequence:

        def own_rows(grads):
            split = grads.reshape(2, n_ctx * rows, wide)
            low = lax.psum_scatter(split, "ctx", scatter_dimension=1, tiled=True)
            return low.reshape(2 * rows, wide)

        dk, dv = own_rows(dk), own_rows(dv)
    up_total = outer(*up_pairs, here_y, add=up_other)
    up_low = scatter(up_total)
    dq = tie(dq, down_low, up_other)
    scaled, inner, gain_sums = unturn(
        place, dq, dk, raw, scales, my_gains, cosine, sine, heads
    )
    spread = jnp.zeros((2, local), f32)
    spread = lax.dynamic_update_slice(spread, gain_sums[:, 0], (jnp.int32(0), first_head))
    gains = jnp.concatenate([spread.reshape(-1), close_a[3] + close_b[3], norm_a[2] + norm_b[2]])
    inner = sum_stats(inner[:, :, 0])
    inner = tie(inner, up_total)[:, :, None] / width
    grad_qkv = norm_back(place, scaled, raw, scales, inner, dv, heads)
    if by_sequence:
        weight_halves = weight.reshape(2, half, 3 * wide)
        weight_mine = lax.dynamic_index_in_dim(weight_halves, here_x, 0, keepdims=False)
        weight_theirs = lax.dynamic_index_in_dim(weight_halves, 1 - here_x, 0, keepdims=False)
        grad_blocks = [grad_qkv[step * rows : (step + 1) * rows] for step in range(n_ctx)]
        theirs = [contract_cols(block, weight_theirs).astype(bf16) for block in grad_blocks]
        others = [swap(block, "tp") for block in theirs]

        def y_half(index, *after):
            tied = tie(grad_qkv, *after)
            return sum(
                contract_rows(
                    lax.dynamic_slice_in_dim(block, index * half, half, axis=1),
                    tied[step * rows : (step + 1) * rows],
                )
                for step, block in enumerate(blocks)
            )

        terms = []
        for step in range(n_ctx):
            block = grad_blocks[step]
            if step == n_ctx - 1:
                block = tie(block, qkv_theirs, gate_low)
            term = contract_cols(block, weight_mine) + others[step].astype(f32)
            if step < n_ctx - 1:
                low = term.astype(bf16)
                term = shift_ctx(low, -1 - step, n_ctx)
                if step == n_ctx - 2:
                    qkv_theirs = y_half(1 - here_y, low, terms[0]).astype(bf16)
            terms.append(term)
        qkv_total = y_half(here_y, qkv_theirs, terms[1]) + swap(qkv_theirs, "y").astype(f32)
        split = qkv_total.reshape(2, n_ctx * piece, 3 * wide)
        mine = lax.dynamic_index_in_dim(split, core, 0, keepdims=False)
        qkv_low = lax.dynamic_index_in_dim(split, 1 - core, 0, keepdims=False)
        qkv_low = (mine + swap(qkv_low.astype(bf16), "core").astype(f32)).astype(bf16)
        received = []
        for step in range(n_ctx):
            start = lax.rem(ctx + step, n_ctx) * piece
            block = lax.dynamic_slice_in_dim(qkv_low, start, piece)
            received.append(shift_ctx(block, step, n_ctx) if step else block)
        terms[-1] = tie(terms[-1], up_low, qkv_low)
        dx = lowered(sum(term.astype(f32) for term in terms))
        dx_rows = beside(here_x, dx, swap(dx, "tp")).astype(f32)
        down_low, gate_low, up_low, out_low = (
            tie(values, dx) for values in (down_low, gate_low, up_low, out_low)
        )
        gains = tie(gains, dx, *received[1:])
        lines = by_source(received, ctx)
        qkv_shards = [
            jnp.concatenate([lines[n, :, c * wide : (c + 1) * wide] for n in range(n_ctx)], axis=1)
            .astype(f32)
            for c in range(3)
        ]
    else:
        grad_rows = [chunk(grad_qkv, j) for j in range(2)]
        token_rows = both(inner_tokens)
        token_rows = [chunk(token_rows, j) for j in range(2)]
        qkv_shards = [
            own_share(
                scatter(
                    outer(
                        token_rows,
                        [r[:, c * wide : (c + 1) * wide] for r in grad_rows],
                        jnp.int32(0),
                        parts=1,
                    ),
                    ("y", "ctx"),
                )
            )
            for c in range(3)
        ]
        sums = [open_sum(contract_cols(rows_part, weight).astype(bf16)) for rows_part in grad_rows]
        dx_rows = reorder(jnp.concatenate([close_sum(*parts) for parts in sums]), outward)
    def late(values):
        return tie(values, theirs[-1]) if by_sequence else values

    grad_tokens = reorder(late(jnp.concatenate([close_a[2], close_b[2]])), outward) + dx_rows

    gains = lax.psum(gains, ("y", "core", "ctx"))
    cuts = [local, 2 * local, 2 * local + width]
    query_gain_grad, key_gain_grad, attn_gain_grad, mlp_gain_grad = jnp.split(gains, cuts)
    attn_gain_grad, mlp_gain_grad = (
        jnp.concatenate([gain[n * piece : (n + 1) * piece] for n in outward])
        for gain in (attn_gain_grad, mlp_gain_grad)
    )
    return (
        reorder(late(jnp.concatenate([norm_a[1], norm_b[1]])), outward),
        grad_tokens,
        *qkv_shards,
        own_share(out_low).T,
        own_share(gate_low),
        own_share(up_low),
        own_share(down_low).T,
        query_gain_grad,
        key_gain_grad,
        attn_gain_grad,
        mlp_gain_grad,
    )


def solution(mesh):
    sizes = {"y": mesh.shape["dp"] // 2, "core": 2, "ctx": mesh.shape["ctx"], "tp": mesh.shape["tp"]}
    split = Mesh(mesh.devices.reshape(tuple(sizes.values())), tuple(sizes))
    dp = ("y", "core")
    every = ("y", "core", "ctx")
    in_specs = (
        P(every, None),
        P(dp),
        P(every, "tp"),
        P(every, "tp"),
        P(every, "tp"),
        P("tp", every),
        P(every, "tp"),
        P(every, "tp"),
        P("tp", every),
        P("tp"),
        P("tp"),
        P(),
        P(),
        P(every, None),
    )
    out_specs = (
        P(every, None),
        P(every, None),
        P(every, "tp"),
        P(every, "tp"),
        P(every, "tp"),
        P("tp", every),
        P(every, "tp"),
        P(every, "tp"),
        P("tp", every),
        P("tp"),
        P("tp"),
        P(),
        P(),
    )
    return jax.shard_map(
        functools.partial(body, sizes=sizes),
        mesh=split,
        in_specs=in_specs,
        out_specs=out_specs,
        check_vma=False,
    )
```

```python
import functools
import math

import jax
import jax.numpy as jnp
from jax import lax
from jax.experimental import pallas as pl
from jax.experimental.pallas import tpu as pltpu
from jax.sharding import Mesh
from jax.sharding import PartitionSpec as P

HD = 128
EPSILON = 1e-06
ROPE_BASE = 500000.0
MASKED = -1e30
SCALING = HD**-0.5
LOG2E = math.log2(math.e)
BLOCK_K = 256
VMEM_LIMIT = 48 << 20
bf16 = jnp.bfloat16
f32 = jnp.float32


def cost(products, moved):
    return pl.CostEstimate(flops=products, bytes_accessed=moved // 2, transcendentals=0)


def dims(left, right, over):
    return lax.dot_general(left, right, (over, ((), ())), preferred_element_type=f32)


def product(left, right):
    return dims(left, right, ((1,), (0,)))


def contract_rows(left, right):
    return dims(left, right, ((0,), (0,)))


def contract_cols(left, right):
    return dims(left, right, ((1,), (1,)))


def key_steps(block, low, high, bk, per_block):
    end = block * per_block
    begin = jnp.minimum(low // bk, end)
    clear = jnp.minimum((high + bk - 1) // bk, end)
    return begin, clear, end


def diagonal(step, scores, start, first, bk):
    key = step * bk + lax.broadcasted_iota(jnp.int32, scores.shape, 0)
    place = step * bk + lax.broadcasted_iota(jnp.int32, scores.shape, 1)
    return jnp.where((key <= place) & (key + first >= start), scores, MASKED)


def attend_kernel(
    first_ref, low_ref, high_ref, start_ref, q_ref, k_ref, v_ref, o_ref, lse_ref, *, bk
):
    size = q_ref.shape[0]
    per_block = size // bk
    block = first_ref[0] + pl.program_id(2)
    sequence = pl.program_id(1)
    queries = q_ref[...]
    start = start_ref[0]

    def update(carry, scores, values):
        peak, total, acc = carry
        new_peak = jnp.maximum(peak, jnp.max(scores, axis=0, keepdims=True))
        weights = jnp.exp2(scores - new_peak)
        shrink = jnp.exp2(peak - new_peak)
        total = total * shrink + jnp.sum(weights, axis=0, keepdims=True)
        acc = acc * shrink + contract_rows(values, weights.astype(bf16))
        return new_peak, total, acc

    def clear_step(j, carry):
        rows = pl.ds(pl.multiple_of(j * bk, bk), bk)
        return update(carry, contract_cols(k_ref[rows, :], queries), v_ref[rows, :])

    def masked_step(j, carry):
        rows = pl.ds(pl.multiple_of(j * bk, bk), bk)
        scores = contract_cols(k_ref[rows, :], queries)
        key = j * bk + lax.broadcasted_iota(jnp.int32, (bk, 1), 0)
        return update(carry, jnp.where(key >= start, scores, MASKED), v_ref[rows, :])

    begin, clear, end = key_steps(
        block, low_ref[sequence, block], high_ref[sequence, block], bk, per_block
    )
    carry = (
        jnp.full((1, size), MASKED, f32),
        jnp.zeros((1, size), f32),
        jnp.zeros((HD, size), f32),
    )
    carry = lax.fori_loop(begin, clear, masked_step, carry)
    carry = lax.fori_loop(jnp.maximum(begin, clear), end, clear_step, carry)
    for step in range(per_block):
        cut = step * bk
        rows = pl.ds(pl.multiple_of(block * size + cut, bk), bk)
        scores = contract_cols(k_ref[rows, :], queries[cut:])
        scores = diagonal(step, scores, start[:, cut:], block * size, bk)
        right = update(tuple(part[:, cut:] for part in carry), scores, v_ref[rows, :])
        if cut:
            right = tuple(
                jnp.concatenate([part[:, :cut], new], axis=1) for part, new in zip(carry, right)
            )
        carry = right
    peak, total, acc = carry
    o_ref[...] = (acc / total).T.astype(bf16)
    lse_ref[0] = peak + jnp.log2(total)


def attend(first, starts, edges, heads, size, query, key, value):
    sequences, length = starts.shape
    slots = query[0].shape[0] // (sequences * size)
    rows = query[0].shape[0]

    def part(offset):
        return pl.BlockSpec((size, HD), lambda g, b, s, *refs: (b * slots + s, offset + g))

    def whole(offset):
        return pl.BlockSpec((length, HD), lambda g, b, s, *refs: (b, offset + g))

    return pl.pallas_call(
        functools.partial(attend_kernel, bk=min(BLOCK_K, size)),
        grid_spec=pltpu.PrefetchScalarGridSpec(
            num_scalar_prefetch=3,
            grid=(heads, sequences, slots),
            in_specs=[
                pl.BlockSpec((1, 1, size), lambda g, b, s, first, *refs: (b, 0, first[0] + s)),
                part(query[1]),
                whole(key[1]),
                whole(value[1]),
            ],
            out_specs=[
                part(0),
                pl.BlockSpec((1, 1, size), lambda g, b, s, *refs: (g, 0, b * slots + s)),
            ],
        ),
        out_shape=[
            jax.ShapeDtypeStruct((rows, heads * HD), bf16),
            jax.ShapeDtypeStruct((heads, 1, rows), f32),
        ],
        cost_estimate=cost(4 * HD * heads * rows * length, 0),
        compiler_params=pltpu.CompilerParams(vmem_limit_bytes=VMEM_LIMIT),
        name="attend",
    )(first, *edges, starts[:, None, :], query[0], key[0], value[0])


def attend_back_kernel(
    first_ref,
    low_ref,
    high_ref,
    start_ref,
    lse_ref,
    q_ref,
    o_ref,
    do_ref,
    k_ref,
    v_ref,
    dq_ref,
    dk_ref,
    dv_ref,
    dk_sum,
    dv_sum,
    *,
    bk,
):
    size = q_ref.shape[0]
    per_block = size // bk
    block = first_ref[0] + pl.program_id(2)
    sequence = pl.program_id(1)
    queries = q_ref[...]
    grads = do_ref[...]
    start = start_ref[0]
    lse = lse_ref[0]
    delta = jnp.sum((grads.astype(f32) * o_ref[...].astype(f32)).T, axis=0, keepdims=True)

    @pl.when(pl.program_id(2) == 0)
    def _():
        dk_sum[...] = jnp.zeros_like(dk_sum)
        dv_sum[...] = jnp.zeros_like(dv_sum)

    def update(dq, scores, rows, cut):
        probs = jnp.exp2(scores - lse[:, cut:])
        dv_sum[rows, :] += product(probs.astype(bf16), grads[cut:])
        dprobs = contract_cols(v_ref[rows, :], grads[cut:])
        dscores = (probs * (dprobs - delta[:, cut:])).astype(bf16)
        dk_sum[rows, :] += product(dscores, queries[cut:])
        return dq + contract_rows(k_ref[rows, :], dscores)

    def clear_step(j, dq):
        rows = pl.ds(pl.multiple_of(j * bk, bk), bk)
        return update(dq, contract_cols(k_ref[rows, :], queries), rows, 0)

    def masked_step(j, dq):
        rows = pl.ds(pl.multiple_of(j * bk, bk), bk)
        scores = contract_cols(k_ref[rows, :], queries)
        key = j * bk + lax.broadcasted_iota(jnp.int32, (bk, 1), 0)
        return update(dq, jnp.where(key >= start, scores, MASKED), rows, 0)

    begin, clear, end = key_steps(
        block, low_ref[sequence, block], high_ref[sequence, block], bk, per_block
    )
    dq = jnp.zeros((HD, size), f32)
    dq = lax.fori_loop(begin, clear, masked_step, dq)
    dq = lax.fori_loop(jnp.maximum(begin, clear), end, clear_step, dq)
    for step in range(per_block):
        cut = step * bk
        rows = pl.ds(pl.multiple_of(block * size + cut, bk), bk)
        scores = contract_cols(k_ref[rows, :], queries[cut:])
        scores = diagonal(step, scores, start[:, cut:], block * size, bk)
        right = update(dq[:, cut:], scores, rows, cut)
        dq = jnp.concatenate([dq[:, :cut], right], axis=1) if cut else right
    dq_ref[...] = (dq.T * SCALING).astype(bf16)

    @pl.when(pl.program_id(2) == pl.num_programs(2) - 1)
    def _():
        dk_ref[...] = (dk_sum[...] * (1.0 / LOG2E)).astype(bf16)
        dv_ref[...] = dv_sum[...].astype(bf16)


def attend_back(first, starts, edges, heads, size, lse, query, out, grad, key, value):
    sequences, length = starts.shape
    rows = query[0].shape[0]
    slots = rows // (sequences * size)

    def part(offset):
        return pl.BlockSpec((size, HD), lambda g, b, s, *refs: (b * slots + s, offset + g))

    def whole(offset):
        return pl.BlockSpec((length, HD), lambda g, b, s, *refs: (b, offset + g))

    return pl.pallas_call(
        functools.partial(attend_back_kernel, bk=min(BLOCK_K, size)),
        grid_spec=pltpu.PrefetchScalarGridSpec(
            num_scalar_prefetch=3,
            grid=(heads, sequences, slots),
            in_specs=[
                pl.BlockSpec((1, 1, size), lambda g, b, s, first, *refs: (b, 0, first[0] + s)),
                pl.BlockSpec((1, 1, size), lambda g, b, s, *refs: (g, 0, b * slots + s)),
                part(query[1]),
                part(0),
                part(0),
                whole(key[1]),
                whole(value[1]),
            ],
            out_specs=[part(0), whole(0), whole(0)],
            scratch_shapes=[pltpu.VMEM((length, HD), f32)] * 2,
        ),
        out_shape=[
            jax.ShapeDtypeStruct((rows, heads * HD), bf16),
            jax.ShapeDtypeStruct((sequences * length, heads * HD), bf16),
            jax.ShapeDtypeStruct((sequences * length, heads * HD), bf16),
        ],
        cost_estimate=cost(5 * HD * heads * rows * length, 0),
        compiler_params=pltpu.CompilerParams(vmem_limit_bytes=VMEM_LIMIT),
        name="attend_back",
    )(first, *edges, starts[:, None, :], lse, query[0], out, grad, key[0], value[0])


def turn_kernel(place_ref, raw_ref, scale_ref, gain_ref, cos_ref, sin_ref, out_ref, *, heads):
    for c in range(3):
        for h in range(heads):
            cols = slice((c * heads + h) * HD, (c * heads + h + 1) * HD)
            values = raw_ref[:, cols]
            if c < 2:
                values = values * scale_ref[c] * gain_ref[c, :, h * HD : (h + 1) * HD]
                values = values * cos_ref[...] + pltpu.roll(values, HD // 2, 1) * sin_ref[...]
            if c == 0:
                values = values * (SCALING * LOG2E)
            out_ref[:, cols] = values.astype(bf16)


def turn(place, raw, scales, gains, cosine, sine, heads):
    rows = raw.shape[0]
    size = rows // place.shape[0]
    return pl.pallas_call(
        functools.partial(turn_kernel, heads=heads),
        grid_spec=pltpu.PrefetchScalarGridSpec(
            num_scalar_prefetch=1,
            grid=(rows // size,),
            in_specs=[
                pl.BlockSpec((size, 3 * heads * HD), lambda i, place: (place[i], 0)),
                pl.BlockSpec((2, size, 1), lambda i, place: (0, i, 0)),
                pl.BlockSpec((2, 1, heads * HD), lambda i, place: (0, 0, 0)),
                pl.BlockSpec((size, HD), lambda i, place: (i, 0)),
                pl.BlockSpec((size, HD), lambda i, place: (i, 0)),
            ],
            out_specs=pl.BlockSpec((size, 3 * heads * HD), lambda i, place: (i, 0)),
        ),
        out_shape=jax.ShapeDtypeStruct(raw.shape, bf16),
        cost_estimate=cost(0, 20 * rows * heads * HD),
        compiler_params=pltpu.CompilerParams(vmem_limit_bytes=VMEM_LIMIT),
        name="turn",
    )(place, raw, scales, gains, cosine, sine)


def unturn_kernel(
    place_ref,
    dq_ref,
    dk_ref,
    raw_ref,
    scale_ref,
    gain_ref,
    cos_ref,
    sin_ref,
    out_ref,
    inner_ref,
    sum_ref,
    *,
    heads,
):
    @pl.when(pl.program_id(0) == 0)
    def _():
        sum_ref[...] = jnp.zeros_like(sum_ref)

    for c, grad_ref in enumerate((dq_ref, dk_ref)):
        inner = 0.0
        for h in range(heads):
            head = slice(h * HD, (h + 1) * HD)
            cols = slice((c * heads + h) * HD, (c * heads + h + 1) * HD)
            grad = grad_ref[:, head].astype(f32)
            normed = grad * cos_ref[...] - pltpu.roll(grad, HD // 2, 1) * sin_ref[...]
            unit = raw_ref[:, cols] * scale_ref[c]
            scaled = normed * gain_ref[c, :, head]
            out_ref[:, cols] = scaled
            inner = inner + jnp.sum(scaled * unit, axis=1, keepdims=True)
            sum_ref[c, :, head] += jnp.sum(normed * unit, axis=0, keepdims=True)
        inner_ref[c] = inner


def unturn(place, dq, dk, raw, scales, gains, cosine, sine, heads):
    rows = raw.shape[0]
    size = rows // place.shape[0]
    width = heads * HD
    return pl.pallas_call(
        functools.partial(unturn_kernel, heads=heads),
        grid_spec=pltpu.PrefetchScalarGridSpec(
            num_scalar_prefetch=1,
            grid=(rows // size,),
            in_specs=[
                pl.BlockSpec((size, width), lambda i, place: (i, 0)),
                pl.BlockSpec((size, width), lambda i, place: (i, 0)),
                pl.BlockSpec((size, 3 * width), lambda i, place: (place[i], 0)),
                pl.BlockSpec((2, size, 1), lambda i, place: (0, i, 0)),
                pl.BlockSpec((2, 1, width), lambda i, place: (0, 0, 0)),
                pl.BlockSpec((size, HD), lambda i, place: (i, 0)),
                pl.BlockSpec((size, HD), lambda i, place: (i, 0)),
            ],
            out_specs=[
                pl.BlockSpec((size, 2 * width), lambda i, place: (i, 0)),
                pl.BlockSpec((2, size, 1), lambda i, place: (0, i, 0)),
                pl.BlockSpec((2, 1, width), lambda i, place: (0, 0, 0)),
            ],
        ),
        out_shape=[
            jax.ShapeDtypeStruct((rows, 2 * width), f32),
            jax.ShapeDtypeStruct((2, rows, 1), f32),
            jax.ShapeDtypeStruct((2, 1, width), f32),
        ],
        cost_estimate=cost(0, 32 * rows * width),
        compiler_params=pltpu.CompilerParams(vmem_limit_bytes=VMEM_LIMIT),
        name="unturn",
    )(place, dq, dk, raw, scales, gains, cosine, sine)


def norm_back_kernel(
    place_ref, scaled_ref, raw_ref, scale_ref, inner_ref, dv_ref, out_ref, *, heads
):
    width = heads * HD
    for c in range(2):
        cols = slice(c * width, (c + 1) * width)
        unit = raw_ref[:, cols] * scale_ref[c]
        out_ref[:, cols] = (scale_ref[c] * (scaled_ref[:, cols] - unit * inner_ref[c])).astype(bf16)
    out_ref[:, 2 * width :] = dv_ref[...]


def norm_back(place, scaled, raw, scales, inner, dv, heads):
    rows = raw.shape[0]
    size = rows // place.shape[0]
    width = heads * HD
    return pl.pallas_call(
        functools.partial(norm_back_kernel, heads=heads),
        grid_spec=pltpu.PrefetchScalarGridSpec(
            num_scalar_prefetch=1,
            grid=(rows // size,),
            in_specs=[
                pl.BlockSpec((size, 2 * width), lambda i, place: (i, 0)),
                pl.BlockSpec((size, 3 * width), lambda i, place: (place[i], 0)),
                pl.BlockSpec((2, size, 1), lambda i, place: (0, i, 0)),
                pl.BlockSpec((2, size, 1), lambda i, place: (0, i, 0)),
                pl.BlockSpec((size, width), lambda i, place: (i, 0)),
            ],
            out_specs=pl.BlockSpec((size, 3 * width), lambda i, place: (place[i], 0)),
        ),
        out_shape=jax.ShapeDtypeStruct((rows, 3 * width), bf16),
        cost_estimate=cost(0, 24 * rows * width),
        compiler_params=pltpu.CompilerParams(vmem_limit_bytes=VMEM_LIMIT),
        name="norm_back",
    )(place, scaled, raw, scales, inner, dv)


def reorder_kernel(in_ref, out_ref, *, order):
    size = in_ref.shape[1] // len(order)
    for n, m in enumerate(order):
        out_ref[:, n * size : (n + 1) * size] = in_ref[:, m * size : (m + 1) * size]


def reorder(values, order):
    rows, width = values.shape
    size = math.gcd(rows, 192)
    spec = pl.BlockSpec((size, width), lambda i: (i, 0))
    return pl.pallas_call(
        functools.partial(reorder_kernel, order=order),
        grid=(rows // size,),
        in_specs=[spec],
        out_specs=spec,
        out_shape=jax.ShapeDtypeStruct(values.shape, values.dtype),
        cost_estimate=cost(0, 2 * values.size * values.dtype.itemsize),
        compiler_params=pltpu.CompilerParams(vmem_limit_bytes=VMEM_LIMIT),
        name="reorder",
    )(values)


def outer_kernel(left_a, left_b, right_a, right_b, out_ref):
    total = contract_rows(left_a[...], right_a[...]) + contract_rows(left_b[...], right_b[...])
    out_ref[...] = total.astype(bf16)


def outer(lefts, rights):
    rows, high = lefts[0].shape
    wide = rights[0].shape[1]
    tall, broad = math.gcd(high, 512), math.gcd(wide, 1024)
    left = pl.BlockSpec((rows, tall), lambda i, j: (0, i))
    right = pl.BlockSpec((rows, broad), lambda i, j: (0, j))
    return pl.pallas_call(
        outer_kernel,
        grid=(high // tall, wide // broad),
        in_specs=[left, left, right, right],
        out_specs=pl.BlockSpec((tall, broad), lambda i, j: (i, j)),
        out_shape=jax.ShapeDtypeStruct((high, wide), bf16),
        cost_estimate=cost(2 * rows * high * wide, 0),
        compiler_params=pltpu.CompilerParams(vmem_limit_bytes=VMEM_LIMIT),
        name="outer",
    )(*lefts, *rights)


def feed_kernel(hidden_ref, gate_ref, up_ref, gate_out, up_out, act_out):
    gate = product(hidden_ref[...], gate_ref[...])
    up = product(hidden_ref[...], up_ref[...])
    gate_out[...] = gate.astype(bf16)
    up_out[...] = up.astype(bf16)
    act_out[...] = (gate * jax.nn.sigmoid(gate) * up).astype(bf16)


def feed(hidden, gate, up_down):
    rows, width = hidden.shape
    units = gate.shape[1]
    wide = math.gcd(units, 512)
    out = pl.BlockSpec((rows, wide), lambda j: (0, j))
    return pl.pallas_call(
        feed_kernel,
        grid=(units // wide,),
        in_specs=[
            pl.BlockSpec((rows, width), lambda j: (0, 0)),
            pl.BlockSpec((width, wide), lambda j: (0, j)),
            pl.BlockSpec((width, wide), lambda j: (0, j)),
        ],
        out_specs=[out, out, out],
        out_shape=[jax.ShapeDtypeStruct((rows, units), bf16)] * 3,
        cost_estimate=cost(2 * rows * width * units, 0),
        compiler_params=pltpu.CompilerParams(vmem_limit_bytes=VMEM_LIMIT),
        name="feed",
    )(hidden, gate, up_down)


def project_kernel(left_ref, right_ref, out_ref):
    out_ref[...] = contract_cols(left_ref[...], right_ref[...]).astype(bf16)


def project(act, up_down):
    rows, units = act.shape
    width = up_down.shape[0]
    wide = math.gcd(width, 512)
    return pl.pallas_call(
        project_kernel,
        grid=(width // wide,),
        in_specs=[
            pl.BlockSpec((rows, units), lambda j: (0, 0)),
            pl.BlockSpec((wide, units), lambda j: (j, 1)),
        ],
        out_specs=pl.BlockSpec((rows, wide), lambda j: (0, j)),
        out_shape=jax.ShapeDtypeStruct((rows, width), bf16),
        cost_estimate=cost(rows * units * width, 0),
        compiler_params=pltpu.CompilerParams(vmem_limit_bytes=VMEM_LIMIT),
        name="project",
    )(act, up_down)


def feed_back_kernel(grad_ref, down_ref, gate_ref, up_ref, gate_out, up_out):
    grad = product(grad_ref[...], down_ref[...])
    gate = gate_ref[...].astype(f32)
    sigmoid = jax.nn.sigmoid(gate)
    gate_out[...] = (
        grad * up_ref[...].astype(f32) * (sigmoid * (1.0 + gate * (1.0 - sigmoid)))
    ).astype(bf16)
    up_out[...] = (grad * (gate * sigmoid)).astype(bf16)


def feed_back(grad, up_down, gate, up):
    rows, width = grad.shape
    units = gate.shape[1]
    wide = math.gcd(units, 512)
    count = units // wide
    part = pl.BlockSpec((rows, wide), lambda j: (0, j))
    return pl.pallas_call(
        feed_back_kernel,
        grid=(count,),
        in_specs=[
            pl.BlockSpec((rows, width), lambda j: (0, 0)),
            pl.BlockSpec((width, wide), lambda j: (0, count + j)),
            part,
            part,
        ],
        out_specs=[part, part],
        out_shape=[jax.ShapeDtypeStruct((rows, units), bf16)] * 2,
        cost_estimate=cost(rows * width * units, 0),
        compiler_params=pltpu.CompilerParams(vmem_limit_bytes=VMEM_LIMIT),
        name="feed_back",
    )(grad, up_down, gate, up)


def project_both_kernel(gate_grad, up_grad, gate_ref, up_ref, out_ref):
    total = contract_cols(gate_grad[...], gate_ref[...]) + contract_cols(up_grad[...], up_ref[...])
    out_ref[...] = total.astype(bf16)


def project_both(gate_grad, up_grad, gate, up_down):
    rows, units = gate_grad.shape
    width = gate.shape[0]
    wide = math.gcd(width, 512)
    left = pl.BlockSpec((rows, units), lambda j: (0, 0))
    return pl.pallas_call(
        project_both_kernel,
        grid=(width // wide,),
        in_specs=[
            left,
            left,
            pl.BlockSpec((wide, units), lambda j: (j, 0)),
            pl.BlockSpec((wide, units), lambda j: (j, 0)),
        ],
        out_specs=pl.BlockSpec((rows, wide), lambda j: (0, j)),
        out_shape=jax.ShapeDtypeStruct((rows, width), bf16),
        cost_estimate=cost(2 * rows * units * width, 0),
        compiler_params=pltpu.CompilerParams(vmem_limit_bytes=VMEM_LIMIT),
        name="project_both",
    )(gate_grad, up_grad, gate, up_down)


def tie_kernel(*refs):
    pass


def tie(values, *others):
    return pl.pallas_call(
        tie_kernel,
        in_specs=[pl.BlockSpec(memory_space=pl.ANY)] * (1 + len(others)),
        out_specs=pl.BlockSpec(memory_space=pl.ANY),
        out_shape=jax.ShapeDtypeStruct(values.shape, values.dtype),
        input_output_aliases={0: 0},
        cost_estimate=cost(0, 0),
        name="tie",
    )(values, *others)


def doc_starts(doc_ids):
    row_index = jnp.arange(doc_ids.shape[-1], dtype=jnp.int32)
    is_start = jnp.concatenate(
        [jnp.ones_like(doc_ids[:, :1], dtype=bool), doc_ids[:, 1:] != doc_ids[:, :-1]], axis=1
    )
    return lax.cummax(jnp.where(is_start, row_index[None, :], 0), axis=1)


def angles(places):
    frequency = ROPE_BASE ** (-(jnp.arange(HD // 2, dtype=f32) * 2.0 / HD))
    phases = places.astype(f32)[:, None] * frequency[None, :]
    cosine, sine = jnp.cos(phases), jnp.sin(phases)
    return (
        jnp.concatenate([cosine, cosine], axis=-1),
        jnp.concatenate([-sine, sine], axis=-1),
    )


def swap(values, axis):
    return lax.ppermute(values, axis, [(0, 1), (1, 0)])


def shift_ctx(values, steps, size):
    return lax.ppermute(values, "ctx", [(i, (i + steps) % size) for i in range(size)])


def by_source(received, me):
    size = len(received)
    turned = jnp.stack(received[::-1] + received[::-1])
    return lax.dynamic_slice_in_dim(turned, size - 1 - me, size, axis=0)


def in_order(index, mine, theirs):
    return jnp.where(index == 0, jnp.stack([mine, theirs]), jnp.stack([theirs, mine]))


def beside(index, mine, theirs):
    first = jnp.where(index == 0, mine, theirs)
    second = jnp.where(index == 0, theirs, mine)
    return jnp.concatenate([first, second], axis=1)


def lowered(values):
    return lax.reduce_precision(values, 8, 7).astype(bf16)


def body(
    tokens,
    segments,
    query_weight,
    key_weight,
    value_weight,
    out_weight,
    gate_weight,
    up_weight,
    down_weight,
    query_gain,
    key_gain,
    attn_gain,
    mlp_gain,
    cotangent,
    *,
    sizes,
):
    core = lax.axis_index("core")
    ctx = lax.axis_index("ctx")
    here_y = lax.axis_index("y")
    here_x = lax.axis_index("tp")
    n_ctx, n_tp = sizes["ctx"], sizes["tp"]
    rows, width = tokens.shape
    piece = query_weight.shape[0]
    local = query_weight.shape[1]
    att = local // 2
    half = width // 2
    short = rows // 2

    def column_half(values, index):
        size = values.shape[1] // 2
        return lax.dynamic_slice_in_dim(values, index * size, size, axis=1)

    def number(y, c, z):
        return (y * 2 + c) * n_ctx + z

    inward = [number(y, c, z) for y in range(2) for z in range(n_ctx) for c in range(2)]
    outward = [inward.index(n) for n in range(4 * n_ctx)]

    def gather(*shards, after=(), axes=("y", "ctx")):
        mine = jnp.concatenate([column_half(shard, core) for shard in shards], axis=1)
        theirs = jnp.concatenate([column_half(shard, 1 - core) for shard in shards], axis=1)
        pair = in_order(core, mine, swap(theirs, "core")).reshape(2 * piece, -1)
        if after:
            pair = tie(pair, *after)
        return lax.all_gather(pair, axes, axis=0, tiled=True)

    def scatter(grad):
        return lax.psum_scatter(grad, ("y", "ctx"), scatter_dimension=0, tiled=True)

    def own_share(low):
        mine = lax.dynamic_slice_in_dim(low, core * piece, piece)
        theirs = swap(lax.dynamic_slice_in_dim(low, (1 - core) * piece, piece), "core")
        return beside(core, mine, theirs).astype(f32)

    def both(values):
        return jnp.concatenate([values, swap(values, "core")], axis=0)

    def open_sum(part):
        part = part.reshape(2, -1, width)
        total = part[0].astype(f32) + swap(part[1], "core").astype(f32)
        if n_tp == 2:
            low = lowered(total)
            return low, swap(low, "tp")
        low = lax.psum(total.astype(bf16), "tp")
        return low, jnp.zeros_like(low)

    def close_sum(low, other):
        return low.astype(f32) + other.astype(f32)

    def chunk(values, j):
        split = values.reshape(2, rows, -1)[:, j * short : (j + 1) * short]
        return split.reshape(2 * short, -1)

    def unchunk(parts):
        split = [part.reshape(2, short, -1) for part in parts]
        return jnp.concatenate(split, axis=1).reshape(2 * rows, -1)

    by_sequence = n_tp == 2 and (local // HD) % n_ctx == 0
    out_all = gather(out_weight.T)
    inner_tokens = reorder(tokens, inward)
    inner_cotangent = reorder(cotangent, inward)
    attn_gain, mlp_gain = (
        jnp.concatenate([gain[n * piece : (n + 1) * piece] for n in inward])
        for gain in (attn_gain, mlp_gain)
    )

    if by_sequence:
        heads = local // HD // n_ctx
        wide = heads * HD

        def shard_columns(index):
            return jnp.concatenate(
                [
                    lax.dynamic_slice_in_dim(shard, index * wide, wide, axis=1)
                    for shard in (query_weight, key_weight, value_weight)
                ],
                axis=1,
            )

        columns = [shard_columns(ctx)]
        for step in range(1, n_ctx):
            columns.append(shift_ctx(shard_columns(lax.rem(ctx + step, n_ctx)), step, n_ctx))
        weight = by_source(columns, ctx).reshape(n_ctx * piece, 3 * wide)
        weight = in_order(core, weight, swap(weight, "core")).reshape(half, 3 * wide)
        weight = in_order(here_y, weight, swap(weight, "y")).reshape(width, 3 * wide)

        sent = lax.dynamic_slice_in_dim(tokens, here_x * short, short)
        blocks = []
        for step in range(1, n_ctx):
            sent = shift_ctx(sent, 1, n_ctx)
            if step == 1:
                sent = tie(sent, *columns[1:])
            elif step == 2:
                sent = tie(sent, weight, blocks[0], out_all)
            blocks.append(in_order(here_x, sent, swap(sent, "tp")).reshape(rows, width))
        blocks.append(tokens)
        raws = [product(block, weight) for block in blocks]
        raw = jnp.concatenate(raws)
        sums = [
            jnp.stack(
                [jnp.sum(jnp.square(r[:, c * wide : (c + 1) * wide]), axis=-1) for c in range(2)]
            )
            for r in raws
        ]
        squares = by_source([sums[-1]] + sums[:-1], ctx).swapaxes(0, 1).reshape(2, n_ctx * rows)
        size = math.gcd(rows, 384)
        order = jnp.arange(n_ctx * rows // size, dtype=jnp.int32)
        block_of, inside = order // (rows // size), order % (rows // size)
        place = lax.rem(ctx - block_of - 1 + n_ctx, n_ctx) * (rows // size) + inside
        place = place.astype(jnp.int32)

        starts = doc_starts(segments[None])
        places = jnp.arange(n_ctx * rows, dtype=jnp.int32) - starts[0]
        first_head = ctx * wide
        first_block = jnp.zeros((1,), jnp.int32)

        def sum_stats(stats):
            return lax.psum(stats, ("ctx", "tp"))

        ready = (sent, blocks[1])
    else:
        heads = att // HD
        wide = att
        weight = gather(query_weight, key_weight, value_weight)
        raw = product(both(inner_tokens), weight)
        ready = ()
        squares = jnp.stack(
            [jnp.sum(jnp.square(raw[:, c * wide : (c + 1) * wide]), axis=-1) for c in range(2)]
        )
        place = jnp.arange(2 * rows // math.gcd(rows, 384), dtype=jnp.int32)
        starts = doc_starts(both(segments[None]))
        here = lax.dynamic_slice_in_dim(starts, ctx * rows, rows, axis=1)
        places = (ctx * rows + jnp.arange(rows, dtype=jnp.int32)[None, :] - here).reshape(-1)
        first_head = core * wide
        first_block = ctx.astype(jnp.int32)[None]

        def sum_stats(stats):
            split = stats.reshape(2, 2, rows)
            ordered = jnp.where(core == 0, split, split[:, ::-1])
            total = lax.psum(ordered, ("core", "tp"))
            return jnp.where(core == 0, total, total[:, ::-1]).reshape(stats.shape)

    gate_line = gather(gate_weight, after=ready, axes="ctx")
    gate_other = swap(gate_line, "y")
    gate_all = in_order(here_y, gate_line, gate_other).reshape(width, -1)
    up_down_all = gather(up_weight, down_weight.T, after=ready)

    my_gains = jnp.stack(
        [
            lax.dynamic_slice_in_dim(query_gain, first_head, wide),
            lax.dynamic_slice_in_dim(key_gain, first_head, wide),
        ]
    )[:, None, :]
    cosine, sine = angles(places)
    edges = starts.reshape(starts.shape[0], n_ctx, rows)
    edges = (edges[:, :, 0], edges[:, :, -1])
    scales = lax.rsqrt(sum_stats(squares) / width + EPSILON)[:, :, None]
    turned = turn(place, raw, scales, my_gains, cosine, sine, heads)
    if by_sequence:
        keys, values = (turned, heads), (turned, 2 * heads)
    else:

        def whole_sequences(columns):
            line = lax.all_gather(columns.reshape(2, rows, wide), "ctx", axis=1, tiled=True)
            return line.reshape(-1, wide)

        keys = (whole_sequences(turned[:, wide : 2 * wide]), 0)
        values = (whole_sequences(turned[:, 2 * wide :]), 0)
    out_att, lse = attend(
        first_block, starts, edges, heads, rows, (turned, 0), keys, values
    )
    if by_sequence:
        received = []
        for step in range(n_ctx):
            start = lax.rem(ctx + step, n_ctx) * rows
            block = lax.dynamic_slice_in_dim(out_att, start, rows)
            received.append(shift_ctx(block, step, n_ctx) if step else block)
        received[-1] = tie(received[-1], gate_other)
        twice = jnp.concatenate(received[::-1] + received[::-1], axis=1)
        own = lax.dynamic_slice_in_dim(twice, (n_ctx - 1 - ctx) * wide, local, axis=1)
        other = swap(lax.dynamic_slice_in_dim(own, (1 - core) * att, att, axis=1), "core")
        attended = jnp.concatenate([lax.dynamic_slice_in_dim(own, core * att, att, axis=1), other])
    else:
        attended = out_att

    spans = [slice(0, short), slice(short, rows)]
    attended = [chunk(attended, j) for j in range(2)]
    parts = [contract_cols(rows_part, out_all).astype(bf16) for rows_part in attended]
    attn_sums = [open_sum(part) for part in parts]

    def forward(j, attn_rows):
        attn_scale = lax.rsqrt(jnp.mean(attn_rows * attn_rows, axis=-1, keepdims=True) + EPSILON)
        attn_unit = attn_rows * attn_scale
        hidden_rows = inner_tokens[spans[j]].astype(f32) + attn_unit * attn_gain
        hidden_low = both(hidden_rows.astype(bf16))
        gate_rows, up_rows, act_low = feed(hidden_low, gate_all, up_down_all)
        part = project(act_low, up_down_all)
        return part, act_low, hidden_low, hidden_rows, attn_scale, attn_unit, gate_rows, up_rows

    def turn_norm(j, state, mlp_rows):
        hidden_rows = state[3]
        mlp_scale = lax.rsqrt(jnp.mean(mlp_rows * mlp_rows, axis=-1, keepdims=True) + EPSILON)
        mlp_unit = mlp_rows * mlp_scale
        output = (hidden_rows + mlp_unit * mlp_gain).astype(bf16)
        grad_out = inner_cotangent[spans[j]].astype(f32)
        gain_part = jnp.sum(grad_out * mlp_unit, axis=0)
        scaled_out = grad_out * mlp_gain
        inner_out = jnp.mean(scaled_out * mlp_unit, axis=-1, keepdims=True)
        grad_mlp_low = both((mlp_scale * (scaled_out - mlp_unit * inner_out)).astype(bf16))
        return grad_mlp_low, output, gain_part

    def turn_back(state, grad_mlp_low):
        gate_rows, up_rows = state[6:]
        grad_gate_low, grad_up_low = feed_back(grad_mlp_low, up_down_all, gate_rows, up_rows)
        back = project_both(grad_gate_low, grad_up_low, gate_all, up_down_all)
        return back, grad_gate_low, grad_up_low

    def close_back(j, state, back_rows):
        attn_scale, attn_unit = state[4], state[5]
        grad_hidden = inner_cotangent[spans[j]].astype(f32) + back_rows
        gain_part = jnp.sum(grad_hidden * attn_unit, axis=0)
        scaled_hidden = grad_hidden * attn_gain
        inner_hidden = jnp.mean(scaled_hidden * attn_unit, axis=-1, keepdims=True)
        grad_attn_low = both((attn_scale * (scaled_hidden - attn_unit * inner_hidden)).astype(bf16))
        grad_att = product(grad_attn_low, out_all).astype(bf16)
        return grad_att, grad_attn_low, grad_hidden, gain_part

    fore_a = forward(0, close_sum(*attn_sums[0]))
    mlp_a = open_sum(fore_a[0])
    fore_b = forward(1, close_sum(attn_sums[1][0], tie(attn_sums[1][1], fore_a[0])))
    mlp_b = open_sum(fore_b[0])
    norm_a = turn_norm(0, fore_a, close_sum(mlp_a[0], tie(mlp_a[1], fore_b[0])))
    back_a = turn_back(fore_a, norm_a[0])
    hid_a = open_sum(back_a[0])
    norm_b = turn_norm(1, fore_b, close_sum(mlp_b[0], tie(mlp_b[1], back_a[0])))
    down_grad = outer((norm_a[0], tie(norm_b[0], hid_a[0])), (fore_a[1], fore_b[1]))
    down_low = scatter(down_grad)
    back_b = turn_back(fore_b, tie(norm_b[0], down_grad))
    hid_b = open_sum(back_b[0])
    hiddens = (fore_a[2], fore_b[2])
    close_a = close_back(0, fore_a, close_sum(hid_a[0], tie(hid_a[1], back_b[0])))
    gate_grad = outer(hiddens, (back_a[1], back_b[1]))
    gate_low = scatter(gate_grad)
    close_b = close_back(1, fore_b, close_sum(hid_b[0], tie(hid_b[1], gate_grad)))
    grad_att = unchunk([close_a[0], close_b[0]])

    def later(values):
        return tie(values, own) if by_sequence else values

    if by_sequence:
        own = beside(core, grad_att[:rows], swap(grad_att[rows:], "core"))
        received = []
        for step in range(n_ctx):
            start = lax.rem(ctx + step, n_ctx) * wide
            block = lax.dynamic_slice_in_dim(own, start, wide, axis=1)
            received.append(shift_ctx(block, step, n_ctx) if step else block)
        grad_att = by_source(received, ctx).reshape(n_ctx * rows, wide)
    up_low = scatter(outer(hiddens, (back_a[2], tie(back_b[2], back_b[0]))))
    out_theirs, out_mine = (
        outer(
            [
                lax.dynamic_slice_in_dim(close[1], index * half, half, axis=1)
                for close in (close_a, close_b)
            ],
            (attended[0], later(attended[1])),
        )
        for index in (1 - here_y, here_y)
    )
    out_total = (out_mine.astype(f32) + swap(out_theirs, "y").astype(f32)).astype(bf16)
    out_sent = []
    for step in range(n_ctx):
        start = lax.rem(ctx + step, n_ctx) * 2 * piece
        block = lax.dynamic_slice_in_dim(out_total, start, 2 * piece)
        out_sent.append(shift_ctx(block, step, n_ctx) if step else block)
    out_low = sum(block.astype(f32) for block in out_sent).astype(bf16)
    dq, dk, dv = attend_back(
        first_block, starts, edges, heads, rows, lse, (turned, 0), out_att, grad_att, keys, values
    )
    if not by_sequence:

        def own_rows(grads):
            split = grads.reshape(2, n_ctx * rows, wide)
            low = lax.psum_scatter(split, "ctx", scatter_dimension=1, tiled=True)
            return low.reshape(2 * rows, wide)

        dk, dv = own_rows(dk), own_rows(dv)
    scaled, inner, gain_sums = unturn(
        place, dq, dk, raw, scales, my_gains, cosine, sine, heads
    )
    inner = sum_stats(inner[:, :, 0])[:, :, None] / width
    grad_qkv = norm_back(place, scaled, raw, scales, inner, dv, heads)

    spread = jnp.zeros((2, local), f32)
    spread = lax.dynamic_update_slice(spread, gain_sums[:, 0], (jnp.int32(0), first_head))
    gains = jnp.concatenate([spread.reshape(-1), close_a[3] + close_b[3], norm_a[2] + norm_b[2]])
    if by_sequence:
        weight_halves = weight.reshape(2, half, 3 * wide)
        weight_mine = lax.dynamic_index_in_dim(weight_halves, here_x, 0, keepdims=False)
        weight_theirs = lax.dynamic_index_in_dim(weight_halves, 1 - here_x, 0, keepdims=False)
        grad_blocks = [grad_qkv[step * rows : (step + 1) * rows] for step in range(n_ctx)]
        theirs = [contract_cols(block, weight_theirs).astype(bf16) for block in grad_blocks]
        others = [swap(block, "tp") for block in theirs]

        def y_half(index, after):
            tied = tie(grad_qkv, after)
            return sum(
                contract_rows(
                    lax.dynamic_slice_in_dim(block, index * half, half, axis=1),
                    tied[step * rows : (step + 1) * rows],
                )
                for step, block in enumerate(blocks)
            )

        terms = []
        for step in range(n_ctx):
            block = grad_blocks[step]
            if step == n_ctx - 1:
                block = tie(block, qkv_theirs)
            other = tie(others[step], terms[0]) if step == 2 else others[step]
            term = contract_cols(block, weight_mine) + other.astype(f32)
            if step < n_ctx - 1:
                low = term.astype(bf16)
                if step == 1:
                    qkv_theirs = y_half(1 - here_y, low).astype(bf16)
                term = shift_ctx(low, -1 - step, n_ctx)
            terms.append(term)
        qkv_total = y_half(here_y, qkv_theirs) + swap(qkv_theirs, "y").astype(f32)
        split = qkv_total.reshape(2, n_ctx * piece, 3 * wide)
        mine = lax.dynamic_index_in_dim(split, core, 0, keepdims=False)
        qkv_low = lax.dynamic_index_in_dim(split, 1 - core, 0, keepdims=False)
        qkv_low = (mine + swap(qkv_low.astype(bf16), "core").astype(f32)).astype(bf16)
        received = []
        for step in range(n_ctx):
            start = lax.rem(ctx + step, n_ctx) * piece
            block = lax.dynamic_slice_in_dim(qkv_low, start, piece)
            received.append(shift_ctx(block, step, n_ctx) if step else block)
        terms[-1] = tie(terms[-1], qkv_low)
        dx = lowered(sum(term.astype(f32) for term in terms))
        dx_rows = beside(here_x, dx, swap(dx, "tp")).astype(f32)
        down_low, gate_low, up_low = (tie(values, dx) for values in (down_low, gate_low, up_low))
        gains = lax.psum(tie(gains, dx, *received[1:]), ("y", "core", "ctx"))
        lines = by_source(received, ctx)
        qkv_shards = [
            jnp.concatenate([lines[n, :, c * wide : (c + 1) * wide] for n in range(n_ctx)], axis=1)
            .astype(f32)
            for c in range(3)
        ]
    else:
        gains = lax.psum(gains, ("y", "core", "ctx"))
        grad_rows = [chunk(grad_qkv, j) for j in range(2)]
        token_rows = both(inner_tokens)
        token_rows = [chunk(token_rows, j) for j in range(2)]
        qkv_shards = [
            own_share(scatter(outer(token_rows, [r[:, c * wide : (c + 1) * wide] for r in grad_rows])))
            for c in range(3)
        ]
        sums = [open_sum(contract_cols(rows_part, weight).astype(bf16)) for rows_part in grad_rows]
        dx_rows = reorder(jnp.concatenate([close_sum(*parts) for parts in sums]), outward)
    def late(values):
        return tie(values, theirs[-1]) if by_sequence else values

    grad_tokens = reorder(late(jnp.concatenate([close_a[2], close_b[2]])), outward) + dx_rows

    cuts = [local, 2 * local, 2 * local + width]
    query_gain_grad, key_gain_grad, attn_gain_grad, mlp_gain_grad = jnp.split(gains, cuts)
    attn_gain_grad, mlp_gain_grad = (
        jnp.concatenate([gain[n * piece : (n + 1) * piece] for n in outward])
        for gain in (attn_gain_grad, mlp_gain_grad)
    )
    return (
        reorder(late(jnp.concatenate([norm_a[1], norm_b[1]])), outward),
        grad_tokens,
        *qkv_shards,
        own_share(out_low).T,
        own_share(gate_low),
        own_share(up_low),
        own_share(down_low).T,
        query_gain_grad,
        key_gain_grad,
        attn_gain_grad,
        mlp_gain_grad,
    )


def solution(mesh):
    sizes = {"y": mesh.shape["dp"] // 2, "core": 2, "ctx": mesh.shape["ctx"], "tp": mesh.shape["tp"]}
    split = Mesh(mesh.devices.reshape(tuple(sizes.values())), tuple(sizes))
    dp = ("y", "core")
    every = ("y", "core", "ctx")
    in_specs = (
        P(every, None),
        P(dp),
        P(every, "tp"),
        P(every, "tp"),
        P(every, "tp"),
        P("tp", every),
        P(every, "tp"),
        P(every, "tp"),
        P("tp", every),
        P("tp"),
        P("tp"),
        P(),
        P(),
        P(every, None),
    )
    out_specs = (
        P(every, None),
        P(every, None),
        P(every, "tp"),
        P(every, "tp"),
        P(every, "tp"),
        P("tp", every),
        P(every, "tp"),
        P(every, "tp"),
        P("tp", every),
        P("tp"),
        P("tp"),
        P(),
        P(),
    )
    return jax.shard_map(
        functools.partial(body, sizes=sizes),
        mesh=split,
        in_specs=in_specs,
        out_specs=out_specs,
        check_vma=False,
    )
```
